128 devices in a mesh: row: 8 (over y_hi, x), col: 16 (over y_lo, z, core).
Axes of the slice: x: 4, y: 4 (y_hi: 2, y_lo: 2; y = y_hi * 2 + y_lo), z: 4, core: 2. Of those that a mesh axis runs over, the one named last changes fastest.
Arguments:
- series: bfloat16 [2048, 6144], P(('row', 'col')), may hold values from -6 to 6
- day_index: int32 [2048], P(('row', 'col')), may hold values from 0 to 364
- lags: int32 [8], replicated, may hold values from -28 to 28, as said below
Outputs:
- covariance: float32 [8, 6144, 6144], P(None, 'row', 'col')
The draws below stay inside these ranges and needn't reach their ends.
Inputs may be any that keep to these rules, and one draw needn't show every extreme that they name: `lags`: both -28 and 28 are in the list.
All inputs are finite; a program needn't handle non-finite values.
Results may differ from the reference program's by a relative error of at most 0.0041.
Values may be sent and summed in bfloat16 or wider, within the bound.
A program may use at most 128 MiB of HBM per device.

```python
import math
import jax
import jax.numpy as jnp
from jax import lax

CHANNELS = 6144
NLAG = 8
MAXLAG = 28
DAYS = 365
TIME = 2048


def draw_lags(key, part):
    key = jax.random.fold_in(key, 7)
    first, second = jax.random.split(key)
    values = jax.random.randint(first, (NLAG,), -MAXLAG, MAXLAG + 1)
    values = values.at[0].set(-MAXLAG).at[1].set(MAXLAG)
    return jax.random.permutation(second, values).astype(jnp.int32)


def set_ends(array, key, smallest, largest):
    place = [jax.random.randint(jax.random.fold_in(key, axis), (), 0, length) for axis, length in enumerate(array.shape)]
    widest = array.shape.index(max(array.shape))
    neighbour = place[:widest] + [(place[widest] + 1) % array.shape[widest]] + place[widest + 1:]
    return array.at[tuple(place)].set(smallest).at[tuple(neighbour)].set(largest)


def steps_of(stream_key, extent, cuts, least, largest):
    loudness = 1.0
    for position, blocks in cuts:
        steps = jax.random.uniform(jax.random.fold_in(jax.random.fold_in(stream_key, 6), position), (blocks,), jnp.float32, least / len(cuts), largest / len(cuts))
        loudness = loudness * jnp.repeat(jnp.exp(steps), extent[position] // blocks).reshape((-1,) + (1,) * (len(extent) - 1 - position))
    return loudness


def noise(key, extent, spread, bound, cuts=(), held_as=jnp.bfloat16):
    drawn = jax.random.normal(key, extent, jnp.float32) * spread
    if len(cuts) > 0:
        drawn = steps_of(key, extent, cuts, -0.22, 0.18) * drawn
    return jnp.clip(drawn, min=-bound, max=bound).astype(held_as)


def setup_inputs(seed: int = 0) -> dict:
    streams_of = jax.random.split(jax.random.key(seed), 4)
    return {
        "series": noise(streams_of[0], (TIME, CHANNELS), 1.0, 6.0, ((0, 128),)),
        "day_index": set_ends(jax.random.randint(streams_of[1], (TIME,), 0, DAYS), jax.random.fold_in(streams_of[1], 1), 0, DAYS - 1).astype(jnp.int32),
        "lags": draw_lags(jax.random.fold_in(streams_of[3], 71), 0),
    }


def reference(series, day_index, lags):
    values = series.astype(jnp.float32)
    day_sums = jax.ops.segment_sum(values, day_index, num_segments=DAYS)
    day_counts = jax.ops.segment_sum(jnp.ones((TIME,), jnp.float32), day_index, num_segments=DAYS)
    climate = day_sums / jnp.maximum(day_counts, 1.0)[:, None]
    steps = jnp.arange(TIME).astype(jnp.float32)
    taper = 0.5 - 0.5 * jnp.cos(2.0 * math.pi * (steps + 0.5) / TIME)
    anomaly = ((values - climate[day_index]) * taper[:, None]).astype(jnp.bfloat16)
    padded = jnp.pad(anomaly, ((MAXLAG, MAXLAG), (0, 0)))

    def one_lag(lag):
        shifted = lax.dynamic_slice_in_dim(padded, (MAXLAG + lag).astype(jnp.int32), TIME, 0)
        prod = lax.dot_general(anomaly, shifted, (((0,), (0,)), ((), ())), preferred_element_type=jnp.float32)
        return prod / TIME

    return lax.map(one_lag, lags)
```

```python
import math

import jax
import jax.numpy as jnp
from jax import lax
from jax.experimental import pallas as pl
from jax.experimental.pallas import tpu as pltpu
from jax.sharding import PartitionSpec as P

NLAG = 8
DAYS = 384
TIME = 2048
NROW = 8
NCOL = 16
NDEV = NROW * NCOL
STEPS = 16
CHANS = 6144
ROWW = 768
COLW = 384
OWN = 48
PAD = 32
MESH = pl.DeviceIdType.MESH
F32 = jnp.float32
BF16 = jnp.bfloat16


class Ring:
    def __init__(self, ref, slot, device, p, q, send, recv):
        self.ref, self.slot, self.device = ref, slot, device
        self.p, self.q, self.send, self.recv = p, q, send, recv
        self.copies = {}

    def at(self, dq):
        return lax.rem(self.q + dq + 4, 4)

    def view(self, slot):
        return self.ref.at[pl.ds(pl.multiple_of(slot * OWN, 16), OWN)]

    def half(self, slot, h):
        lanes = pl.ds(h * (TIME // 2), TIME // 2)
        return self.ref.at[pl.ds(pl.multiple_of(slot * OWN, 16), OWN), lanes]

    def copy(self, n, ref, dev):
        copy = pltpu.make_async_remote_copy(
            src_ref=ref,
            dst_ref=ref,
            send_sem=self.send.at[n],
            recv_sem=self.recv.at[n],
            device_id=dev,
            device_id_type=MESH,
        )
        copy.start()
        self.copies[n] = copy

    def own(self):
        ref = self.view(self.slot(self.p, self.q))
        self.copy(1, ref, self.device(self.p, self.at(1)))
        self.copy(2, ref, self.device(self.p, self.at(-1)))
        self.copy(0, ref, self.device(1 - self.p, self.q))

    def other(self):
        self.copies[0].wait_recv()
        ref = self.view(self.slot(1 - self.p, self.q))
        self.copy(3, ref, self.device(self.p, self.at(1)))
        self.copy(4, ref, self.device(self.p, self.at(-1)))

    def forward(self, n):
        self.copies[n].wait_recv()
        pair = self.p if n < 3 else 1 - self.p
        if n % 2 == 1:
            ref = self.half(self.slot(pair, self.at(-1)), 0)
            self.copy(n + 4, ref, self.device(self.p, self.at(1)))
        else:
            ref = self.half(self.slot(pair, self.at(1)), 1)
            self.copy(n + 4, ref, self.device(self.p, self.at(-1)))


def dot(a, b):
    return jnp.dot(a, b, preferred_element_type=F32)


def split(x):
    high = x.astype(BF16)
    return high, (x - high.astype(F32)).astype(BF16)


def pick(held, start, to, lane):
    tile, off = divmod(start, 128)
    first = held[:, tile * 128 : (tile + 1) * 128].astype(F32)
    got = pltpu.roll(first, (to - off) % 128, 1)
    if off + OWN > 128:
        second = held[:, (tile + 1) * 128 : (tile + 2) * 128].astype(F32)
        got = jnp.where(lane < to + 128 - off, got, pltpu.roll(second, (to - off) % 128, 1))
    return got


def gather_kernel(
    series, days, lags, at, pad, lagv,
    held, held_days, held_lags, stage, land, xt, onehot, bt,
    sl, ss, rs, sra, rra, srb, rrb, ssib, rsib,
):
    r = lax.axis_index("row")
    c = lax.axis_index("col")
    rank = r * NCOL + c
    loads = [
        pltpu.make_async_copy(series, held, sl.at[0]),
        pltpu.make_async_copy(days, held_days, sl.at[1]),
        pltpu.make_async_copy(lags, held_lags, sl.at[2]),
    ]
    for load in loads:
        load.start()
    barrier = pltpu.get_barrier_semaphore()

    @pl.loop(1, NDEV)
    def _(j):
        to = lax.rem(rank + j, NDEV)
        pl.semaphore_signal(barrier, inc=1, device_id=(to // NCOL, lax.rem(to, NCOL)), device_id_type=MESH)

    for load in loads:
        load.wait()
    step = lax.broadcasted_iota(jnp.int32, (STEPS, 128), 0)
    lane = lax.broadcasted_iota(jnp.int32, (STEPS, 128), 1)
    day = jnp.zeros((STEPS, 128), jnp.int32)
    for i in range(STEPS):
        day = jnp.where(step == i, held_days[i], day)
    high = jnp.right_shift(day, 8)
    info = jnp.where(lane == 96, high, jnp.where(lane == 97, day - high * 256, jnp.where(lane == 98, 1, 0)))
    info = info.astype(F32)
    for d in range(NDEV):
        mine = pick(held, OWN * d, 0, lane)
        theirs = pick(held, COLW * (d % NCOL) + OWN * (d // NCOL), OWN, lane)
        row = jnp.where(lane < OWN, mine, jnp.where(lane < 2 * OWN, theirs, info))
        stage[d] = row.astype(BF16)
    for k in range(NLAG):
        lagv[k : k + 1, :] = jnp.full((1, 128), held_lags[k], jnp.int32).astype(F32)

    pl.semaphore_wait(barrier, NDEV - 1)

    @pl.loop(1, NDEV)
    def _(j):
        to = lax.rem(rank + j, NDEV)
        pltpu.make_async_remote_copy(
            src_ref=stage.at[to],
            dst_ref=land.at[rank],
            send_sem=ss,
            recv_sem=rs,
            device_id=(to // NCOL, lax.rem(to, NCOL)),
            device_id_type=MESH,
        ).start()

    land[rank] = stage[rank]
    when = lax.broadcasted_iota(jnp.int32, (NCOL, 128), 0) * 128 + lax.broadcasted_iota(jnp.int32, (NCOL, 128), 1)
    taper = 0.5 - 0.5 * jnp.cos(2.0 * math.pi * (when.astype(F32) + 0.5) / TIME)
    pad[:, :PAD, :] = jnp.zeros((3, PAD, 128), F32)
    pad[:, PAD + TIME :, :] = jnp.zeros((3, PAD, 128), F32)
    everyone = pltpu.make_async_remote_copy(
        src_ref=stage.at[0 : NDEV - 1],
        dst_ref=land.at[0 : NDEV - 1],
        send_sem=ss,
        recv_sem=rs,
        device_id=(r, c),
        device_id_type=MESH,
    )
    everyone.wait_recv()

    down = lax.broadcasted_iota(jnp.int32, (DAYS, 128), 0).astype(F32)
    for k in range(NCOL):
        here = land[8 * k : 8 * k + 8].reshape(128, 128).astype(F32).T
        lanes = slice(k * 128, (k + 1) * 128)
        xt[:, lanes] = here[: 2 * OWN]
        day_row = here[96:97] * 256.0 + here[97:98]
        onehot[:, lanes] = jnp.where(down == day_row, 1.0, 0.0).astype(BF16)
    sums = dot(onehot[...], land[...].reshape(TIME, 128))
    climate = sums * (1.0 / jnp.maximum(sums[:, 98:99], 1.0))
    high, low = split(climate.T[: 2 * OWN])
    both = jnp.concatenate([high, low], axis=0)
    for n in range(4):
        season = dot(both, onehot[:, n * 512 : (n + 1) * 512])
        season = season[: 2 * OWN] + season[2 * OWN :]
        for i in range(4):
            k = 4 * n + i
            lanes = slice(k * 128, (k + 1) * 128)
            anomaly = (xt[:, lanes] - season[:, i * 128 : (i + 1) * 128]) * taper[k : k + 1]
            anomaly = anomaly.astype(BF16)
            at[pl.ds(pl.multiple_of(c * OWN, 16), OWN), lanes] = anomaly[:OWN]
            bt[pl.ds(pl.multiple_of(r * OWN, 16), OWN), lanes] = anomaly[OWN:]

    core = lax.rem(c, 2)
    ring_a = Ring(
        at,
        lambda p, q: p * 8 + q * 2 + core,
        lambda p, q: (r, p * 8 + q * 2 + core),
        c // 8,
        lax.rem(c // 2, 4),
        sra,
        rra,
    )
    ring_b = Ring(
        bt,
        lambda p, q: p * 4 + q,
        lambda p, q: (p * 4 + q, c),
        r // 4,
        lax.rem(r, 4),
        srb,
        rrb,
    )
    siblings = []

    def sibling(p, q):
        n = len(siblings)
        ref = ring_a.view(ring_a.slot(p, q))
        copy = pltpu.make_async_remote_copy(
            src_ref=ref,
            dst_ref=ref,
            send_sem=ssib.at[n],
            recv_sem=rsib.at[n],
            device_id=(r, c + 1 - 2 * core),
            device_id_type=MESH,
        )
        copy.start()
        siblings.append(copy)

    ring_a.own()
    ring_b.own()
    pa, qa = ring_a.p, ring_a.q
    sibling(pa, qa)
    ring_a.other()
    ring_b.other()
    for n in (1, 2):
        ring_a.forward(n)
        ring_b.forward(n)
    sibling(1 - pa, qa)
    sibling(pa, ring_a.at(-1))
    sibling(pa, ring_a.at(1))
    for n in (3, 4):
        ring_a.forward(n)
        ring_b.forward(n)
    sibling(1 - pa, ring_a.at(-1))
    sibling(1 - pa, ring_a.at(1))
    for n in (5, 6):
        ring_a.copies[n].wait_recv()
    sibling(pa, ring_a.at(2))
    for n in (7, 8):
        ring_a.copies[n].wait_recv()
    sibling(1 - pa, ring_a.at(2))
    for n in (5, 6, 7, 8):
        ring_b.copies[n].wait_recv()
    for w in range(3):
        for k in range(NCOL):
            tile = bt[w * 128 : (w + 1) * 128, k * 128 : (k + 1) * 128].astype(F32)
            pad[w, PAD + k * 128 : PAD + (k + 1) * 128, :] = tile.T
    for copy in siblings:
        copy.wait()
    everyone.wait_send()
    for copy in list(ring_a.copies.values()) + list(ring_b.copies.values()):
        copy.wait_send()


def gather(series, day_index, lags):
    dma = pltpu.SemaphoreType.DMA
    hbm = pl.BlockSpec(memory_space=pltpu.HBM)
    vmem = pl.BlockSpec(memory_space=pltpu.VMEM)
    return pl.pallas_call(
        gather_kernel,
        out_shape=(
            jax.ShapeDtypeStruct((ROWW, TIME), BF16),
            jax.ShapeDtypeStruct((3, TIME + 2 * PAD, 128), F32),
            jax.ShapeDtypeStruct((NLAG, 128), F32),
        ),
        in_specs=[hbm, hbm, hbm],
        out_specs=(vmem, vmem, vmem),
        scratch_shapes=[
            pltpu.VMEM((STEPS, CHANS), BF16),
            pltpu.SMEM((STEPS,), jnp.int32),
            pltpu.SMEM((NLAG,), jnp.int32),
            pltpu.VMEM((NDEV, STEPS, 128), BF16),
            pltpu.VMEM((NDEV, STEPS, 128), BF16),
            pltpu.VMEM((2 * OWN, TIME), F32),
            pltpu.VMEM((DAYS, TIME), BF16),
            pltpu.VMEM((COLW, TIME), BF16),
            dma((3,)),
            dma(()),
            dma(()),
            dma((9,)),
            dma((9,)),
            dma((9,)),
            dma((9,)),
            dma((8,)),
            dma((8,)),
        ],
        compiler_params=pltpu.CompilerParams(
            collective_id=0, has_side_effects=True, vmem_limit_bytes=24 * 2**20
        ),
        name="gather_anomaly",
    )(series, day_index, lags)


def cov_kernel(at, pad, lagv, out, even, odd):
    g = pl.program_id(0)
    m = pl.program_id(1)

    def fill(pair, first, count, held):
        for i in range(2):
            lag = jnp.max(lagv[pl.ds(2 * pair + i, 1), :]).astype(jnp.int32)
            for w in range(3):
                lanes = slice(i * COLW + w * 128, i * COLW + (w + 1) * 128)
                piece = pad[w, pl.ds(first + PAD + lag, count), :]
                held[pl.ds(first, count), lanes] = piece.astype(BF16)

    @pl.when((g == 0) & (m == 0))
    def _():
        fill(0, 0, TIME, even)

    def body(now, later):
        fill(lax.rem(g + 1, NLAG // 2), pl.multiple_of(m * (TIME // 2), TIME // 2), TIME // 2, later)
        prod = dot(at[pl.ds(pl.multiple_of(m * 384, 384), 384), :], now[...]) * (1.0 / TIME)
        out[0] = prod[:, :COLW]
        out[1] = prod[:, COLW:]

    @pl.when(lax.rem(g, 2) == 0)
    def _():
        body(even, odd)

    @pl.when(lax.rem(g, 2) == 1)
    def _():
        body(odd, even)


def covariance(at, pad, lagv):
    once = pl.Buffered(1)
    return pl.pallas_call(
        cov_kernel,
        grid=(NLAG // 2, 2),
        out_shape=jax.ShapeDtypeStruct((NLAG, ROWW, COLW), F32),
        in_specs=[
            pl.BlockSpec((ROWW, TIME), lambda g, m: (0, 0), pipeline_mode=once),
            pl.BlockSpec((3, TIME + 2 * PAD, 128), lambda g, m: (0, 0, 0), pipeline_mode=once),
            pl.BlockSpec((NLAG, 128), lambda g, m: (0, 0), pipeline_mode=once),
        ],
        out_specs=pl.BlockSpec((2, ROWW // 2, COLW), lambda g, m: (g, m, 0)),
        scratch_shapes=[
            pltpu.VMEM((TIME, 2 * COLW), BF16),
            pltpu.VMEM((TIME, 2 * COLW), BF16),
        ],
        compiler_params=pltpu.CompilerParams(
            dimension_semantics=("arbitrary", "arbitrary"), vmem_limit_bytes=36 * 2**20
        ),
        name="lagged_covariance",
    )(at, pad, lagv)


def shards(series, day_index, lags):
    return covariance(*gather(series, day_index, lags))


def solution(mesh):
    placed = (P(("row", "col"), None), P(("row", "col")), P())
    return jax.shard_map(
        shards, mesh=mesh, in_specs=placed, out_specs=P(None, "row", "col"), check_vma=False
    )
```

```python
import math

import jax
import jax.numpy as jnp
from jax import lax
from jax.experimental import pallas as pl
from jax.experimental.pallas import tpu as pltpu
from jax.sharding import PartitionSpec as P

NLAG = 8
DAYS = 384
TIME = 2048
NROW = 8
NCOL = 16
NDEV = NROW * NCOL
STEPS = 16
CHANS = 6144
ROWW = 768
COLW = 384
OWN = 48
PAD = 32
CHUNKS = ((0, 640), (640, 512), (1152, 512), (1664, 384))
HALVES = (384, 256, 256, 128)
WINDOW = 512
PAIRS = NLAG // 2
MESH = pl.DeviceIdType.MESH
F32 = jnp.float32
BF16 = jnp.bfloat16


class Ring:
    def __init__(self, ref, slot, device, p, q, send, recv):
        self.ref, self.slot, self.device = ref, slot, device
        self.p, self.q, self.send, self.recv = p, q, send, recv
        self.copies = {}

    def at(self, dq):
        return lax.rem(self.q + dq + 4, 4)

    def view(self, slot, j, half=None):
        start, size = CHUNKS[j]
        if half == 0:
            size = HALVES[j]
        elif half == 1:
            start, size = start + HALVES[j], size - HALVES[j]
        return self.ref.at[pl.ds(pl.multiple_of(slot * OWN, 16), OWN), start : start + size]

    def copy(self, j, n, ref, dev):
        copy = pltpu.make_async_remote_copy(
            src_ref=ref,
            dst_ref=ref,
            send_sem=self.send.at[j, n],
            recv_sem=self.recv.at[j, n],
            device_id=dev,
            device_id_type=MESH,
        )
        copy.start()
        self.copies[j, n] = copy

    def across(self, j):
        self.copy(j, 0, self.view(self.slot(self.p, self.q), j), self.device(1 - self.p, self.q))

    def own(self, j):
        ref = self.view(self.slot(self.p, self.q), j)
        self.copy(j, 1, ref, self.device(self.p, self.at(1)))
        self.copy(j, 2, ref, self.device(self.p, self.at(-1)))

    def other(self, j):
        self.copies[j, 0].wait_recv()
        ref = self.view(self.slot(1 - self.p, self.q), j)
        self.copy(j, 3, ref, self.device(self.p, self.at(1)))
        self.copy(j, 4, ref, self.device(self.p, self.at(-1)))

    def forward(self, j, n):
        self.copies[j, n].wait_recv()
        pair = self.p if n < 3 else 1 - self.p
        if n % 2 == 1:
            self.copy(j, n + 4, self.view(self.slot(pair, self.at(-1)), j, 0), self.device(self.p, self.at(1)))
        else:
            self.copy(j, n + 4, self.view(self.slot(pair, self.at(1)), j, 1), self.device(self.p, self.at(-1)))


def fill(pad, lag, i, first, count, held):
    for w in range(3):
        piece = pad[w, pl.ds(first + PAD + lag, count), :]
        held[:, i * COLW + w * 128 : i * COLW + (w + 1) * 128] = piece.astype(BF16)


def dot(a, b):
    return jnp.dot(a, b, preferred_element_type=F32)


def split(x):
    high = x.astype(BF16)
    return high, (x - high.astype(F32)).astype(BF16)


def pick(held, start, to, lane):
    tile, off = divmod(start, 128)
    first = held[:, tile * 128 : (tile + 1) * 128].astype(F32)
    got = pltpu.roll(first, (to - off) % 128, 1)
    if off + OWN > 128:
        second = held[:, (tile + 1) * 128 : (tile + 2) * 128].astype(F32)
        got = jnp.where(lane < to + 128 - off, got, pltpu.roll(second, (to - off) % 128, 1))
    return got


def gather_kernel(
    series, days, lags, at, pad, lagv, part,
    held, held_days, held_lags, stage, land, xt, onehot, bt, even, odd,
    sl, ss, rs, sra, rra, srb, rrb, ssib, rsib,
):
    r = lax.axis_index("row")
    c = lax.axis_index("col")
    rank = r * NCOL + c
    loads = [
        pltpu.make_async_copy(series, held, sl.at[0]),
        pltpu.make_async_copy(days, held_days, sl.at[1]),
        pltpu.make_async_copy(lags, held_lags, sl.at[2]),
    ]
    for load in loads:
        load.start()
    barrier = pltpu.get_barrier_semaphore()

    @pl.loop(1, NDEV)
    def _(j):
        to = lax.rem(rank + j, NDEV)
        pl.semaphore_signal(barrier, inc=1, device_id=(to // NCOL, lax.rem(to, NCOL)), device_id_type=MESH)

    for load in loads:
        load.wait()
    step = lax.broadcasted_iota(jnp.int32, (STEPS, 128), 0)
    lane = lax.broadcasted_iota(jnp.int32, (STEPS, 128), 1)
    day = jnp.zeros((STEPS, 128), jnp.int32)
    for i in range(STEPS):
        day = jnp.where(step == i, held_days[i], day)
    high = jnp.right_shift(day, 8)
    info = jnp.where(lane == 96, high, jnp.where(lane == 97, day - high * 256, jnp.where(lane == 98, 1, 0)))
    info = info.astype(F32)
    for d in range(NDEV):
        mine = pick(held, OWN * d, 0, lane)
        theirs = pick(held, COLW * (d % NCOL) + OWN * (d // NCOL), OWN, lane)
        row = jnp.where(lane < OWN, mine, jnp.where(lane < 2 * OWN, theirs, info))
        stage[d] = row.astype(BF16)
    for k in range(NLAG):
        lagv[k : k + 1, :] = jnp.full((1, 128), held_lags[k], jnp.int32).astype(F32)

    pl.semaphore_wait(barrier, NDEV - 1)

    @pl.loop(1, NDEV)
    def _(j):
        to = lax.rem(rank + j, NDEV)
        pltpu.make_async_remote_copy(
            src_ref=stage.at[to],
            dst_ref=land.at[rank],
            send_sem=ss,
            recv_sem=rs,
            device_id=(to // NCOL, lax.rem(to, NCOL)),
            device_id_type=MESH,
        ).start()

    land[rank] = stage[rank]
    when = lax.broadcasted_iota(jnp.int32, (NCOL, 128), 0) * 128 + lax.broadcasted_iota(jnp.int32, (NCOL, 128), 1)
    taper = 0.5 - 0.5 * jnp.cos(2.0 * math.pi * (when.astype(F32) + 0.5) / TIME)
    pad[:, :PAD, :] = jnp.zeros((3, PAD, 128), F32)
    pad[:, PAD + TIME :, :] = jnp.zeros((3, PAD, 128), F32)
    everyone = pltpu.make_async_remote_copy(
        src_ref=stage.at[0 : NDEV - 1],
        dst_ref=land.at[0 : NDEV - 1],
        send_sem=ss,
        recv_sem=rs,
        device_id=(r, c),
        device_id_type=MESH,
    )
    everyone.wait_recv()

    down = lax.broadcasted_iota(jnp.int32, (DAYS, 128), 0).astype(F32)
    for k in range(NCOL):
        here = land[8 * k : 8 * k + 8].reshape(128, 128).astype(F32).T
        lanes = slice(k * 128, (k + 1) * 128)
        xt[:, lanes] = here[: 2 * OWN]
        day_row = here[96:97] * 256.0 + here[97:98]
        onehot[:, lanes] = jnp.where(down == day_row, 1.0, 0.0).astype(BF16)
    sums = dot(onehot[...], land[...].reshape(TIME, 128))
    climate = sums * (1.0 / jnp.maximum(sums[:, 98:99], 1.0))
    high, low = split(climate.T[: 2 * OWN])
    both = jnp.concatenate([high, low], axis=0)
    for n in range(4):
        season = dot(both, onehot[:, n * 512 : (n + 1) * 512])
        season = season[: 2 * OWN] + season[2 * OWN :]
        for i in range(4):
            k = 4 * n + i
            lanes = slice(k * 128, (k + 1) * 128)
            anomaly = (xt[:, lanes] - season[:, i * 128 : (i + 1) * 128]) * taper[k : k + 1]
            anomaly = anomaly.astype(BF16)
            at[pl.ds(pl.multiple_of(c * OWN, 16), OWN), lanes] = anomaly[:OWN]
            bt[pl.ds(pl.multiple_of(r * OWN, 16), OWN), lanes] = anomaly[OWN:]

    core = lax.rem(c, 2)
    ring_a = Ring(
        at,
        lambda p, q: p * 8 + q * 2 + core,
        lambda p, q: (r, p * 8 + q * 2 + core),
        c // 8,
        lax.rem(c // 2, 4),
        sra,
        rra,
    )
    ring_b = Ring(
        bt,
        lambda p, q: p * 4 + q,
        lambda p, q: (p * 4 + q, c),
        r // 4,
        lax.rem(r, 4),
        srb,
        rrb,
    )
    siblings = {}
    pa, qa = ring_a.p, ring_a.q

    def sibling(j, p, q):
        n = sum(key[0] == j for key in siblings)
        ref = ring_a.view(ring_a.slot(p, q), j)
        copy = pltpu.make_async_remote_copy(
            src_ref=ref,
            dst_ref=ref,
            send_sem=ssib.at[j, n],
            recv_sem=rsib.at[j, n],
            device_id=(r, c + 1 - 2 * core),
            device_id_type=MESH,
        )
        copy.start()
        siblings[j, n] = copy

    def own(j):
        ring_a.own(j)
        ring_b.own(j)
        sibling(j, pa, qa)

    def other(j):
        ring_a.other(j)
        ring_b.other(j)
        sibling(j, 1 - pa, qa)

    def near(j):
        for n in (1, 2):
            ring_a.forward(j, n)
            ring_b.forward(j, n)
        sibling(j, pa, ring_a.at(-1))
        sibling(j, pa, ring_a.at(1))

    def far(j):
        for n in (3, 4):
            ring_a.forward(j, n)
            ring_b.forward(j, n)
        sibling(j, 1 - pa, ring_a.at(-1))
        sibling(j, 1 - pa, ring_a.at(1))

    def last(j):
        for n, p in ((5, pa), (7, 1 - pa)):
            ring_a.copies[j, n].wait_recv()
            ring_a.copies[j, n + 1].wait_recv()
            sibling(j, p, ring_a.at(2))
        for n in (5, 6, 7, 8):
            ring_b.copies[j, n].wait_recv()

    def turn(j):
        start, size = CHUNKS[j]
        for w in range(3):
            for k in range(start, start + size, 128):
                tile = bt[w * 128 : (w + 1) * 128, k : k + 128].astype(F32)
                pad[w, PAD + k : PAD + k + 128, :] = tile.T

    def close(j):
        for n in range(8):
            siblings[j, n].wait_recv()

    def products(j, between):
        first = j * WINDOW
        for i in range(2):
            fill(pad, held_lags[i], i, first, WINDOW, even)
        for n in range(2 * PAIRS):
            pair, m = n // 2, n % 2
            now, later = (even, odd) if pair % 2 == 0 else (odd, even)
            if pair + 1 < PAIRS:
                fill(pad, held_lags[2 * pair + 2 + m], m, first, WINDOW, later)
            prod = dot(at[m * 384 : (m + 1) * 384, first : first + WINDOW], now[...])
            for i in range(2):
                where = (2 * pair + i, slice(m * 384, (m + 1) * 384))
                here = prod[:, i * COLW : (i + 1) * COLW]
                part[where] = here if j == 0 else part[where] + here
            for act in between.get(n, ()):
                act()

    for j in range(4):
        ring_a.across(j)
        ring_b.across(j)
    own(0)
    own(1)
    near(0)
    other(0)
    own(2)
    near(1)
    far(0)
    own(3)
    other(1)
    last(0)
    turn(0)
    close(0)
    products(
        0,
        {
            0: [lambda: near(2)],
            2: [lambda: far(1)],
            3: [lambda: other(2)],
            5: [lambda: near(3)],
            6: [lambda: last(1)],
        },
    )
    turn(1)
    close(1)
    products(1, {1: [lambda: far(2)], 3: [lambda: other(3)], 5: [lambda: last(2)]})
    turn(2)
    close(2)
    products(2, {2: [lambda: far(3)], 6: [lambda: last(3)]})
    turn(3)
    close(3)
    everyone.wait_send()
    for copy in list(siblings.values()) + list(ring_a.copies.values()) + list(ring_b.copies.values()):
        copy.wait_send()


def gather(series, day_index, lags):
    dma = pltpu.SemaphoreType.DMA
    hbm = pl.BlockSpec(memory_space=pltpu.HBM)
    vmem = pl.BlockSpec(memory_space=pltpu.VMEM)
    return pl.pallas_call(
        gather_kernel,
        out_shape=(
            jax.ShapeDtypeStruct((ROWW, TIME), BF16),
            jax.ShapeDtypeStruct((3, TIME + 2 * PAD, 128), F32),
            jax.ShapeDtypeStruct((NLAG, 128), F32),
            jax.ShapeDtypeStruct((NLAG, ROWW, COLW), F32),
        ),
        in_specs=[hbm, hbm, hbm],
        out_specs=(vmem, vmem, vmem, vmem),
        scratch_shapes=[
            pltpu.VMEM((STEPS, CHANS), BF16),
            pltpu.SMEM((STEPS,), jnp.int32),
            pltpu.SMEM((NLAG,), jnp.int32),
            pltpu.VMEM((NDEV, STEPS, 128), BF16),
            pltpu.VMEM((NDEV, STEPS, 128), BF16),
            pltpu.VMEM((2 * OWN, TIME), F32),
            pltpu.VMEM((DAYS, TIME), BF16),
            pltpu.VMEM((COLW, TIME), BF16),
            pltpu.VMEM((WINDOW, 2 * COLW), BF16),
            pltpu.VMEM((WINDOW, 2 * COLW), BF16),
            dma((3,)),
            dma(()),
            dma(()),
            dma((4, 9)),
            dma((4, 9)),
            dma((4, 9)),
            dma((4, 9)),
            dma((4, 8)),
            dma((4, 8)),
        ],
        compiler_params=pltpu.CompilerParams(
            collective_id=0, has_side_effects=True, vmem_limit_bytes=24 * 2**20
        ),
        name="gather_anomaly",
    )(*(pltpu.with_memory_space_constraint(x, pltpu.HBM) for x in (series, day_index, lags)))


def cov_kernel(at, pad, lagv, part, out, even, odd):
    first = TIME - WINDOW
    g = pl.program_id(0)
    m = pl.program_id(1)

    def shift(pair, i, held):
        lag = jnp.max(lagv[pl.ds(2 * pair + i, 1), :]).astype(jnp.int32)
        fill(pad, lag, i, first, WINDOW, held)

    @pl.when((g == 0) & (m == 0))
    def _():
        shift(0, 0, even)
        shift(0, 1, even)

    def body(now, later):
        for i in range(2):

            @pl.when(m == i)
            def _():
                shift(lax.rem(g + 1, PAIRS), i, later)
                rows = slice(i * 384, (i + 1) * 384)
                prod = dot(at[rows, first:], now[...])
                out[0] = (part[2 * g, rows] + prod[:, :COLW]) * (1.0 / TIME)
                out[1] = (part[2 * g + 1, rows] + prod[:, COLW:]) * (1.0 / TIME)

    @pl.when(lax.rem(g, 2) == 0)
    def _():
        body(even, odd)

    @pl.when(lax.rem(g, 2) == 1)
    def _():
        body(odd, even)


def covariance(at, pad, lagv, part):
    vmem = pl.BlockSpec(memory_space=pltpu.VMEM)
    return pl.pallas_call(
        cov_kernel,
        grid=(PAIRS, 2),
        out_shape=jax.ShapeDtypeStruct((NLAG, ROWW, COLW), F32),
        in_specs=[vmem] * 4,
        out_specs=pl.BlockSpec((2, ROWW // 2, COLW), lambda g, m: (g, m, 0)),
        scratch_shapes=[
            pltpu.VMEM((WINDOW, 2 * COLW), BF16),
            pltpu.VMEM((WINDOW, 2 * COLW), BF16),
        ],
        compiler_params=pltpu.CompilerParams(
            dimension_semantics=("arbitrary", "arbitrary"), vmem_limit_bytes=20 * 2**20
        ),
        name="lagged_covariance",
    )(at, pad, lagv, part)


def shards(series, day_index, lags):
    return covariance(*gather(series, day_index, lags))


def solution(mesh):
    placed = (P(("row", "col"), None), P(("row", "col")), P())
    return jax.shard_map(
        shards, mesh=mesh, in_specs=placed, out_specs=P(None, "row", "col"), check_vma=False
    )
```

```python
import math

import jax
import jax.numpy as jnp
from jax import lax
from jax.experimental import pallas as pl
from jax.experimental.pallas import tpu as pltpu
from jax.sharding import PartitionSpec as P

NLAG = 8
DAYS = 384
TIME = 2048
NROW = 8
NCOL = 16
NDEV = NROW * NCOL
NPAIR = NCOL // 2
NCHIP = NDEV // 2
STEPS = 16
CHANS = 6144
ROWW = 768
COLW = 384
OWN = 48
PAD = 32
CHUNKS = ((0, 1152), (1152, 896))
HALVES = (640, 384)
WINDOW = 1024
PAIRS = NLAG // 2
SLOTS = 3
MESH = pl.DeviceIdType.MESH
F32 = jnp.float32
BF16 = jnp.bfloat16


class Ring:
    def __init__(self, ref, slot, device, p, q, send, recv):
        self.ref, self.slot, self.device = ref, slot, device
        self.p, self.q, self.send, self.recv = p, q, send, recv
        self.copies = {}

    def at(self, dq):
        return lax.rem(self.q + dq + 4, 4)

    def view(self, slot, j, half=None):
        start, size = CHUNKS[j]
        if half == 0:
            size = HALVES[j]
        elif half == 1:
            start, size = start + HALVES[j], size - HALVES[j]
        return self.ref.at[pl.ds(pl.multiple_of(slot * OWN, 16), OWN), start : start + size]

    def copy(self, j, n, ref, dev):
        copy = pltpu.make_async_remote_copy(
            src_ref=ref,
            dst_ref=ref,
            send_sem=self.send.at[j, n],
            recv_sem=self.recv.at[j, n],
            device_id=dev,
            device_id_type=MESH,
        )
        copy.start()
        self.copies[j, n] = copy

    def across(self, j):
        self.copy(j, 0, self.view(self.slot(self.p, self.q), j), self.device(1 - self.p, self.q))

    def own(self, j):
        ref = self.view(self.slot(self.p, self.q), j)
        self.copy(j, 1, ref, self.device(self.p, self.at(1)))
        self.copy(j, 2, ref, self.device(self.p, self.at(-1)))

    def other(self, j):
        self.copies[j, 0].wait_recv()
        ref = self.view(self.slot(1 - self.p, self.q), j)
        self.copy(j, 3, ref, self.device(self.p, self.at(1)))
        self.copy(j, 4, ref, self.device(self.p, self.at(-1)))

    def forward(self, j, n):
        self.copies[j, n].wait_recv()
        pair = self.p if n < 3 else 1 - self.p
        if n % 2 == 1:
            self.copy(j, n + 4, self.view(self.slot(pair, self.at(-1)), j, 0), self.device(self.p, self.at(1)))
        else:
            self.copy(j, n + 4, self.view(self.slot(pair, self.at(1)), j, 1), self.device(self.p, self.at(-1)))


def fill(pad, lag, i, first, count, held):
    for w in range(3):
        piece = pad[w, pl.ds(first + PAD + lag, count), :]
        held[:, i * COLW + w * 128 : i * COLW + (w + 1) * 128] = piece.astype(BF16)


def dot(a, b):
    return jnp.dot(a, b, preferred_element_type=F32)


def split(x):
    high = x.astype(BF16)
    return high, (x - high.astype(F32)).astype(BF16)


def pick(held, start, to, lane):
    tile, off = divmod(start, 128)
    first = held[:, tile * 128 : (tile + 1) * 128].astype(F32)
    got = pltpu.roll(first, (to - off) % 128, 1)
    if off + OWN > 128:
        second = held[:, (tile + 1) * 128 : (tile + 2) * 128].astype(F32)
        got = jnp.where(lane < to + 128 - off, got, pltpu.roll(second, (to - off) % 128, 1))
    return got


def gather_kernel(
    series, days, lags, at, pad, lagv, part,
    held, held_days, held_lags, stage, mid, land, xt, onehot, bt, even, odd,
    sl, ss, rs, sx, rx, sra, rra, srb, rrb, ssib, rsib,
):
    r = lax.axis_index("row")
    c = lax.axis_index("col")
    core = lax.rem(c, 2)
    chip = r * NPAIR + c // 2
    to_r = [jnp.where(r + j >= NROW, r + j - NROW, r + j) for j in range(NROW)]
    to_c = [jnp.where(c + 2 * j >= NCOL, c + 2 * j - NCOL, c + 2 * j) for j in range(NPAIR)]
    to_p = [jnp.where(c // 2 + j >= NPAIR, c // 2 + j - NPAIR, c // 2 + j) for j in range(NPAIR)]
    across = (r, c + 1 - 2 * core)
    loads = [
        pltpu.make_async_copy(series, held, sl.at[0]),
        pltpu.make_async_copy(days, held_days, sl.at[1]),
        pltpu.make_async_copy(lags, held_lags, sl.at[2]),
    ]
    for load in loads:
        load.start()
    barrier = pltpu.get_barrier_semaphore()

    for jr in range(NROW):
        for jc in range(NPAIR):
            if jr or jc:
                pl.semaphore_signal(barrier, inc=1, device_id=(to_r[jr], to_c[jc]), device_id_type=MESH)
    pl.semaphore_signal(barrier, inc=1, device_id=across, device_id_type=MESH)

    for load in loads:
        load.wait()
    step = lax.broadcasted_iota(jnp.int32, (STEPS, 128), 0)
    lane = lax.broadcasted_iota(jnp.int32, (STEPS, 128), 1)
    day = jnp.zeros((STEPS, 128), jnp.int32)
    for i in range(STEPS):
        day = jnp.where(step == i, held_days[i], day)
    high = jnp.right_shift(day, 8)
    info = jnp.where(lane == 96, high, jnp.where(lane == 97, day - high * 256, jnp.where(lane == 98, 1, 0)))
    info = info.astype(F32)
    for d in range(NDEV):
        mine = pick(held, OWN * d, 0, lane)
        theirs = pick(held, COLW * (d % NCOL) + OWN * (d // NCOL), OWN, lane)
        row = jnp.where(lane < OWN, mine, jnp.where(lane < 2 * OWN, theirs, info))
        stage[d // 2, d % 2] = row.astype(BF16)
    for k in range(NLAG):
        lagv[k : k + 1, :] = jnp.full((1, 128), held_lags[k], jnp.int32).astype(F32)

    pl.semaphore_wait(barrier, NCHIP)
    for jr in range(NROW):
        for jc in range(NPAIR):
            if jr or jc:
                pltpu.make_async_remote_copy(
                    src_ref=stage.at[to_r[jr] * NPAIR + to_p[jc]],
                    dst_ref=mid.at[chip],
                    send_sem=ss,
                    recv_sem=rs,
                    device_id=(to_r[jr], to_c[jc]),
                    device_id_type=MESH,
                ).start()
    mid[chip] = stage[chip]
    when = lax.broadcasted_iota(jnp.int32, (NCOL, 128), 0) * 128 + lax.broadcasted_iota(jnp.int32, (NCOL, 128), 1)
    taper = 0.5 - 0.5 * jnp.cos(2.0 * math.pi * (when.astype(F32) + 0.5) / TIME)
    pad[:, :PAD, :] = jnp.zeros((3, PAD, 128), F32)
    pad[:, PAD + TIME :, :] = jnp.zeros((3, PAD, 128), F32)
    everyone = pltpu.make_async_remote_copy(
        src_ref=stage.at[0 : NCHIP - 1],
        dst_ref=mid.at[0 : NCHIP - 1],
        send_sem=ss,
        recv_sem=rs,
        device_id=across,
        device_id_type=MESH,
    )
    everyone.wait_recv()
    swap = pltpu.make_async_remote_copy(
        src_ref=mid.at[:, 1 - core],
        dst_ref=land.at[:, core],
        send_sem=sx,
        recv_sem=rx,
        device_id=across,
        device_id_type=MESH,
    )
    swap.start()
    land[:, pl.ds(core, 1)] = mid[:, pl.ds(core, 1)]
    swap.wait_recv()

    down = lax.broadcasted_iota(jnp.int32, (DAYS, 128), 0).astype(F32)
    for k in range(NCOL):
        here = land[4 * k : 4 * k + 4].reshape(128, 128).astype(F32).T
        lanes = slice(k * 128, (k + 1) * 128)
        xt[:, lanes] = here[: 2 * OWN]
        day_row = here[96:97] * 256.0 + here[97:98]
        onehot[:, lanes] = jnp.where(down == day_row, 1.0, 0.0).astype(BF16)
    sums = dot(onehot[...], land[...].reshape(TIME, 128))
    climate = sums * (1.0 / jnp.maximum(sums[:, 98:99], 1.0))
    high, low = split(climate.T[: 2 * OWN])
    both = jnp.concatenate([high, low], axis=0)
    for n in range(4):
        season = dot(both, onehot[:, n * 512 : (n + 1) * 512])
        season = season[: 2 * OWN] + season[2 * OWN :]
        for i in range(4):
            k = 4 * n + i
            lanes = slice(k * 128, (k + 1) * 128)
            anomaly = (xt[:, lanes] - season[:, i * 128 : (i + 1) * 128]) * taper[k : k + 1]
            anomaly = anomaly.astype(BF16)
            at[pl.ds(pl.multiple_of(c * OWN, 16), OWN), lanes] = anomaly[:OWN]
            bt[pl.ds(pl.multiple_of(r * OWN, 16), OWN), lanes] = anomaly[OWN:]

    ring_a = Ring(
        at,
        lambda p, q: p * 8 + q * 2 + core,
        lambda p, q: (r, p * 8 + q * 2 + core),
        c // 8,
        lax.rem(c // 2, 4),
        sra,
        rra,
    )
    ring_b = Ring(
        bt,
        lambda p, q: p * 4 + q,
        lambda p, q: (p * 4 + q, c),
        r // 4,
        lax.rem(r, 4),
        srb,
        rrb,
    )
    siblings = {}
    pa, qa = ring_a.p, ring_a.q

    def sibling(j, p, q):
        n = sum(key[0] == j for key in siblings)
        ref = ring_a.view(ring_a.slot(p, q), j)
        copy = pltpu.make_async_remote_copy(
            src_ref=ref,
            dst_ref=ref,
            send_sem=ssib.at[j, n],
            recv_sem=rsib.at[j, n],
            device_id=across,
            device_id_type=MESH,
        )
        copy.start()
        siblings[j, n] = copy

    def own(j):
        ring_a.own(j)
        ring_b.own(j)
        sibling(j, pa, qa)

    def other(j):
        ring_a.other(j)
        ring_b.other(j)
        sibling(j, 1 - pa, qa)

    def near(j):
        for n in (1, 2):
            ring_a.forward(j, n)
            ring_b.forward(j, n)
        sibling(j, pa, ring_a.at(-1))
        sibling(j, pa, ring_a.at(1))

    def far(j):
        for n in (3, 4):
            ring_a.forward(j, n)
            ring_b.forward(j, n)
        sibling(j, 1 - pa, ring_a.at(-1))
        sibling(j, 1 - pa, ring_a.at(1))

    def last(j):
        for n, p in ((5, pa), (7, 1 - pa)):
            ring_a.copies[j, n].wait_recv()
            ring_a.copies[j, n + 1].wait_recv()
            sibling(j, p, ring_a.at(2))
        for n in (5, 6, 7, 8):
            ring_b.copies[j, n].wait_recv()

    def turn(j):
        start, size = CHUNKS[j]
        for w in range(3):
            for k in range(start, start + size, 128):
                tile = bt[w * 128 : (w + 1) * 128, k : k + 128].astype(F32)
                pad[w, PAD + k : PAD + k + 128, :] = tile.T

    def close(j):
        for n in range(8):
            siblings[j, n].wait_recv()

    def products(j, between):
        first = j * WINDOW
        for i in range(2):
            fill(pad, held_lags[i], i, first, WINDOW, even)
        for n in range(2 * PAIRS):
            pair, m = n // 2, n % 2
            now, later = (even, odd) if pair % 2 == 0 else (odd, even)
            if pair + 1 < PAIRS:
                fill(pad, held_lags[2 * pair + 2 + m], m, first, WINDOW, later)
            rows = slice(m * 384, (m + 1) * 384)
            part[pair, rows] = dot(at[rows, first : first + WINDOW], now[...])
            for act in between.get(n, ()):
                act()

    ring_a.across(0)
    ring_b.across(0)
    own(0)
    ring_a.across(1)
    ring_b.across(1)
    near(0)
    own(1)
    other(0)
    far(0)
    last(0)
    turn(0)
    close(0)
    products(
        0,
        {
            0: [lambda: near(1)],
            2: [lambda: other(1)],
            4: [lambda: far(1)],
            6: [lambda: last(1)],
        },
    )
    turn(1)
    close(1)
    swap.wait_send()
    everyone.wait_send()
    for copy in list(siblings.values()) + list(ring_a.copies.values()) + list(ring_b.copies.values()):
        copy.wait_send()


def gather(series, day_index, lags):
    dma = pltpu.SemaphoreType.DMA
    hbm = pl.BlockSpec(memory_space=pltpu.HBM)
    vmem = pl.BlockSpec(memory_space=pltpu.VMEM)
    return pl.pallas_call(
        gather_kernel,
        out_shape=(
            jax.ShapeDtypeStruct((ROWW, TIME), BF16),
            jax.ShapeDtypeStruct((3, TIME + 2 * PAD, 128), F32),
            jax.ShapeDtypeStruct((NLAG, 128), F32),
            jax.ShapeDtypeStruct((PAIRS, ROWW, 2 * COLW), F32),
        ),
        in_specs=[hbm, hbm, hbm],
        out_specs=(vmem, vmem, vmem, vmem),
        scratch_shapes=[
            pltpu.VMEM((STEPS, CHANS), BF16),
            pltpu.SMEM((STEPS,), jnp.int32),
            pltpu.SMEM((NLAG,), jnp.int32),
            pltpu.VMEM((NCHIP, 2, STEPS, 128), BF16),
            pltpu.VMEM((NCHIP, 2, STEPS, 128), BF16),
            pltpu.VMEM((NCHIP, 2, STEPS, 128), BF16),
            pltpu.VMEM((2 * OWN, TIME), F32),
            pltpu.VMEM((DAYS, TIME), BF16),
            pltpu.VMEM((COLW, TIME), BF16),
            pltpu.VMEM((WINDOW, 2 * COLW), BF16),
            pltpu.VMEM((WINDOW, 2 * COLW), BF16),
            dma((3,)),
            dma(()),
            dma(()),
            dma(()),
            dma(()),
            dma((2, 9)),
            dma((2, 9)),
            dma((2, 9)),
            dma((2, 9)),
            dma((2, 8)),
            dma((2, 8)),
        ],
        compiler_params=pltpu.CompilerParams(
            collective_id=0, has_side_effects=True, vmem_limit_bytes=24 * 2**20
        ),
        name="gather_anomaly",
    )(*(pltpu.with_memory_space_constraint(x, pltpu.HBM) for x in (series, day_index, lags)))


def cov_kernel(at, pad, lagv, part, out, even, odd, done, sems):
    first = TIME - WINDOW
    lag = [jnp.max(lagv[k : k + 1, :]).astype(jnp.int32) for k in range(NLAG)]
    for i in range(2):
        fill(pad, lag[i], i, first, WINDOW, even)
    copies = []
    for n in range(2 * PAIRS):
        pair, m = n // 2, n % 2
        now, later = (even, odd) if pair % 2 == 0 else (odd, even)
        slot = n % SLOTS
        if n >= SLOTS:
            copies[n - SLOTS].wait()
        if pair + 1 < PAIRS:
            fill(pad, lag[2 * pair + 2 + m], m, first, WINDOW, later)
        rows = slice(m * 384, (m + 1) * 384)
        total = (part[pair, rows] + dot(at[rows, first:], now[...])) * (1.0 / TIME)
        for i in range(2):
            done[slot, i] = total[:, i * COLW : (i + 1) * COLW]
        copy = pltpu.make_async_copy(done.at[slot], out.at[2 * pair : 2 * pair + 2, rows], sems.at[slot])
        copy.start()
        copies.append(copy)
    for copy in copies[-SLOTS:]:
        copy.wait()


def covariance(at, pad, lagv, part):
    vmem = pl.BlockSpec(memory_space=pltpu.VMEM)
    return pl.pallas_call(
        cov_kernel,
        out_shape=jax.ShapeDtypeStruct((NLAG, ROWW, COLW), F32),
        in_specs=[vmem] * 4,
        out_specs=pl.BlockSpec(memory_space=pltpu.HBM),
        scratch_shapes=[
            pltpu.VMEM((WINDOW, 2 * COLW), BF16),
            pltpu.VMEM((WINDOW, 2 * COLW), BF16),
            pltpu.VMEM((SLOTS, 2, 384, COLW), F32),
            pltpu.SemaphoreType.DMA((SLOTS,)),
        ],
        compiler_params=pltpu.CompilerParams(vmem_limit_bytes=20 * 2**20),
        name="lagged_covariance",
    )(at, pad, lagv, part)


def shards(series, day_index, lags):
    return covariance(*gather(series, day_index, lags))


def solution(mesh):
    placed = (P(("row", "col"), None), P(("row", "col")), P())
    return jax.shard_map(
        shards, mesh=mesh, in_specs=placed, out_specs=P(None, "row", "col"), check_vma=False
    )
```

```python
import math

import jax
import jax.numpy as jnp
from jax import lax
from jax.experimental import pallas as pl
from jax.experimental.pallas import tpu as pltpu
from jax.sharding import PartitionSpec as P

NLAG = 8
DAYS = 384
TIME = 2048
NROW = 8
NCOL = 16
STEPS = 16
ROWW = 768
COLW = 384
EXT = ROWW + 16
PAD = 32
CHANS = 6144
GROUP = 4
NPART = 4
PART = ROWW // NPART
SLOTS = 3
MESH = pl.DeviceIdType.MESH
F32 = jnp.float32
BF16 = jnp.bfloat16


class Ring:
    def __init__(self, view, half, slot, device, p, q, send, recv):
        self.view, self.half, self.slot, self.device = view, half, slot, device
        self.p, self.q, self.send, self.recv = p, q, send, recv
        self.copies = {}

    def at(self, dq):
        return lax.rem(self.q + dq + 4, 4)

    def copy(self, n, ref, dev):
        copy = pltpu.make_async_remote_copy(
            src_ref=ref,
            dst_ref=ref,
            send_sem=self.send.at[n],
            recv_sem=self.recv.at[n],
            device_id=dev,
            device_id_type=MESH,
        )
        copy.start()
        self.copies[n] = copy

    def own(self):
        ref = self.view(self.slot(self.p, self.q))
        self.copy(1, ref, self.device(self.p, self.at(1)))
        self.copy(2, ref, self.device(self.p, self.at(-1)))
        self.copy(0, ref, self.device(1 - self.p, self.q))

    def other(self):
        self.copies[0].wait_recv()
        ref = self.view(self.slot(1 - self.p, self.q))
        self.copy(3, ref, self.device(self.p, self.at(1)))
        self.copy(4, ref, self.device(self.p, self.at(-1)))

    def forward(self, n):
        self.copies[n].wait_recv()
        pair = self.p if n < 3 else 1 - self.p
        if n % 2 == 1:
            ref = self.half(self.slot(pair, self.at(-1)), 0)
            self.copy(n + 4, ref, self.device(self.p, self.at(1)))
        else:
            ref = self.half(self.slot(pair, self.at(1)), 1)
            self.copy(n + 4, ref, self.device(self.p, self.at(-1)))


def gather_kernel(
    series, days, lags, at, bp, lagv,
    held, held_days, held_lags, stage, land, sl, sa, ra, sb, rb, sra, rra, srb, rrb, ssib, rsib,
):
    r = lax.axis_index("row")
    c = lax.axis_index("col")
    loads = [
        pltpu.make_async_copy(series, held, sl.at[0]),
        pltpu.make_async_copy(days, held_days, sl.at[1]),
        pltpu.make_async_copy(lags, held_lags, sl.at[2]),
    ]
    for load in loads:
        load.start()
    barrier = pltpu.get_barrier_semaphore()
    for j in range(1, NROW):
        pl.semaphore_signal(barrier, inc=1, device_id=(lax.rem(r + j, NROW), c), device_id_type=MESH)
    for j in range(1, NCOL):
        pl.semaphore_signal(barrier, inc=1, device_id=(r, lax.rem(c + j, NCOL)), device_id_type=MESH)

    for load in loads:
        load.wait()
    step = lax.broadcasted_iota(jnp.int32, (STEPS, 128), 0)
    lane = lax.broadcasted_iota(jnp.int32, (STEPS, 128), 1)
    day = jnp.zeros((STEPS, 128), jnp.int32)
    for i in range(STEPS):
        day = jnp.where(step == i, held_days[i], day)
    high = jnp.right_shift(day, 8)
    info = jnp.where(lane == 0, high, jnp.where(lane == 1, day - high * 256, 0))
    info = info.astype(F32).astype(BF16)
    for d in range(NROW):
        stage[d, :, :ROWW] = held[:, d * ROWW : (d + 1) * ROWW]
        stage[d, :, ROWW:] = info

    for k in range(NLAG):
        lagv[k : k + 1, :] = jnp.full((1, 128), held_lags[k], jnp.int32).astype(F32)
    pl.semaphore_wait(barrier, NROW + NCOL - 2)

    rows, cols = [], []
    for j in range(1, NROW):
        to = lax.rem(r + j, NROW)
        copy = pltpu.make_async_remote_copy(
            src_ref=stage.at[to],
            dst_ref=land.at[r],
            send_sem=sa.at[j],
            recv_sem=ra.at[j],
            device_id=(to, c),
            device_id_type=MESH,
        )
        copy.start()
        rows.append(copy)
    for j in range(1, NCOL):
        to = lax.rem(c + j, NCOL)
        copy = pltpu.make_async_remote_copy(
            src_ref=held.at[:, pl.ds(pl.multiple_of(to * COLW, 128), COLW)],
            dst_ref=bp.at[c, r],
            send_sem=sb.at[j],
            recv_sem=rb.at[j],
            device_id=(r, to),
            device_id_type=MESH,
        )
        copy.start()
        cols.append(copy)
    land[r] = stage[r]
    bp[c, r] = held[:, pl.ds(pl.multiple_of(c * COLW, 128), COLW)]

    core = lax.rem(c, 2)
    ring_a = Ring(
        lambda s: at.at[s],
        lambda s, h: at.at[s, 400 * h : 400 + 384 * h],
        lambda p, q: p * 8 + q * 2 + core,
        lambda p, q: (r, p * 8 + q * 2 + core),
        c // 8,
        lax.rem(c // 2, 4),
        sra,
        rra,
    )
    ring_b = Ring(
        lambda s: bp.at[:, s],
        lambda s, h: bp.at[8 * h : 8 * h + 8, s],
        lambda p, q: p * 4 + q,
        lambda p, q: (p * 4 + q, c),
        r // 4,
        lax.rem(r, 4),
        srb,
        rrb,
    )
    siblings = []

    def sibling(p, q):
        n = len(siblings)
        ref = at.at[ring_a.slot(p, q)]
        copy = pltpu.make_async_remote_copy(
            src_ref=ref,
            dst_ref=ref,
            send_sem=ssib.at[n],
            recv_sem=rsib.at[n],
            device_id=(r, c + 1 - 2 * core),
            device_id_type=MESH,
        )
        copy.start()
        siblings.append(copy)

    for copy in rows:
        copy.wait_recv()
    block = land[...].reshape(NROW * STEPS, ROWW + 128).astype(F32)
    at[c] = block.T[:EXT].astype(BF16)
    ring_a.own()
    for copy in cols:
        copy.wait_recv()
    ring_b.own()
    pa, qa = ring_a.p, ring_a.q
    sibling(pa, qa)
    ring_a.other()
    ring_b.other()
    ring_a.forward(1)
    ring_a.forward(2)
    ring_b.forward(1)
    ring_b.forward(2)
    sibling(1 - pa, qa)
    sibling(pa, ring_a.at(-1))
    sibling(pa, ring_a.at(1))
    ring_a.forward(3)
    ring_a.forward(4)
    ring_b.forward(3)
    ring_b.forward(4)
    sibling(1 - pa, ring_a.at(-1))
    sibling(1 - pa, ring_a.at(1))
    for pair, first in ((pa, 5), (1 - pa, 7)):
        ring_a.copies[first].wait_recv()
        ring_a.copies[first + 1].wait_recv()
        sibling(pair, ring_a.at(2))
    for n in (5, 6, 7, 8):
        ring_b.copies[n].wait_recv()
    for copy in siblings:
        copy.wait()
    for copy in rows + cols + list(ring_a.copies.values()) + list(ring_b.copies.values()):
        copy.wait_send()


def hbm(x):
    return pltpu.with_memory_space_constraint(x, pltpu.HBM)


HBM = pl.BlockSpec(memory_space=pltpu.HBM)
VMEM = pl.BlockSpec(memory_space=pltpu.VMEM)
DMA = pltpu.SemaphoreType.DMA


def gather(series, day_index, lags):
    return pl.pallas_call(
        gather_kernel,
        out_shape=(
            jax.ShapeDtypeStruct((NCOL, EXT, 128), BF16),
            jax.ShapeDtypeStruct((NCOL, NROW, STEPS, COLW), BF16),
            jax.ShapeDtypeStruct((NLAG, 128), F32),
        ),
        in_specs=[HBM, HBM, HBM],
        out_specs=(VMEM, VMEM, VMEM),
        scratch_shapes=[
            pltpu.VMEM((STEPS, CHANS), BF16),
            pltpu.SMEM((STEPS,), jnp.int32),
            pltpu.SMEM((NLAG,), jnp.int32),
            pltpu.VMEM((NROW, STEPS, ROWW + 128), BF16),
            pltpu.VMEM((NROW, STEPS, ROWW + 128), BF16),
            DMA((3,)),
            DMA((NROW,)),
            DMA((NROW,)),
            DMA((NCOL,)),
            DMA((NCOL,)),
            DMA((9,)),
            DMA((9,)),
            DMA((9,)),
            DMA((9,)),
            DMA((8,)),
            DMA((8,)),
        ],
        compiler_params=pltpu.CompilerParams(
            collective_id=0, has_side_effects=True, vmem_limit_bytes=8 * 2**20
        ),
        name="gather_series",
    )(hbm(series), hbm(day_index), hbm(lags))


def fill(pad, lag, i, held):
    for k in range(NCOL):
        for b in range(NROW):
            to = (k * NROW + b) * 16
            for w in range(3):
                piece = pad[w, pl.ds(PAD + b * 256 + k * 16 + lag, 16), :]
                held[to : to + 16, i * COLW + w * 128 : i * COLW + (w + 1) * 128] = piece.astype(BF16)


def dot(a, b):
    return jnp.dot(a, b, preferred_element_type=F32)


def split(x):
    high = x.astype(BF16)
    return high, (x - high.astype(F32)).astype(BF16)


def cov_kernel(lagv, at, bp, out, anom, onehot, onehot_t, pad, early, late, done, sems):
    lag = [jnp.max(lagv[k : k + 1, :]).astype(jnp.int32) for k in range(NLAG)]
    place = lax.broadcasted_iota(jnp.int32, (NCOL, 128), 1)
    when = place // STEPS * (NCOL * STEPS) + lax.broadcasted_iota(jnp.int32, (NCOL, 128), 0) * STEPS + place % STEPS
    taper = 0.5 - 0.5 * jnp.cos(2.0 * math.pi * (when.astype(F32) + 0.5) / TIME)
    taper_t = taper.T

    info = at[:, ROWW:, :].astype(F32)
    day = info[:, 0, :] * 256.0 + info[:, 1, :]
    day_t = day.T
    down = lax.broadcasted_iota(jnp.int32, (DAYS, 128), 0).astype(F32)
    along = lax.broadcasted_iota(jnp.int32, (128, DAYS), 1).astype(F32)
    count = jnp.zeros((DAYS, 128), F32)
    for k in range(NCOL):
        steps = slice(k * 128, (k + 1) * 128)
        here = jnp.where(down == day[k : k + 1, :], 1.0, 0.0)
        count = count + here
        hot = here.astype(BF16)
        onehot[:DAYS, steps] = hot
        onehot[DAYS:, steps] = hot
        hot = jnp.where(along == day_t[:, k : k + 1], 1.0, 0.0).astype(BF16)
        onehot_t[steps, :DAYS] = hot
        onehot_t[steps, DAYS:] = hot
    inv_col = 1.0 / jnp.maximum(jnp.sum(count, axis=1, keepdims=True), 1.0)
    inv_row = jnp.broadcast_to(inv_col, (DAYS, 128)).T[0:1, :]

    sums = dot(onehot[:DAYS, :], bp[...].reshape(TIME, COLW))
    both = jnp.concatenate(split(sums * inv_col), axis=0)
    pad[:, :PAD, :] = jnp.zeros((3, PAD, 128), F32)
    pad[:, PAD + TIME :, :] = jnp.zeros((3, PAD, 128), F32)
    for q in range(4):
        season = dot(onehot_t[q * 512 : (q + 1) * 512, :], both)
        for k in range(4 * q, 4 * q + 4):
            here = bp[k].reshape(128, COLW).astype(F32) - season[(k - 4 * q) * 128 : (k - 4 * q + 1) * 128]
            here = (here * taper_t[:, k : k + 1]).astype(BF16).astype(F32)
            for b in range(NROW):
                row = PAD + b * 256 + k * 16
                for w in range(3):
                    pad[w, row : row + 16, :] = here[b * 16 : (b + 1) * 16, w * 128 : (w + 1) * 128]

    for m in range(3):
        rows = slice(m * 256, (m + 1) * 256)
        block = jnp.concatenate([at[k, rows, :] for k in range(NCOL)], axis=1)
        sums = lax.dot_general(block, onehot[:DAYS, :], (((1,), (1,)), ((), ())), preferred_element_type=F32)
        both = jnp.concatenate(split(sums * inv_row), axis=1)
        for k in range(GROUP):
            if k % 3 == m:
                fill(pad, lag[k], k, early)
        for n in range(2):
            season = dot(both, onehot[:, n * 1024 : (n + 1) * 1024])
            for i in range(8):
                k = 8 * n + i
                here = at[k, rows, :].astype(F32) - season[:, i * 128 : (i + 1) * 128]
                anom[rows, k * 128 : (k + 1) * 128] = (here * taper[k : k + 1, :]).astype(BF16)

    copies = []
    for n in range(2 * NPART):
        group, m = divmod(n, NPART)
        slot = n % SLOTS
        if n >= SLOTS:
            copies[n - SLOTS].wait()
        if group == 0:
            fill(pad, lag[GROUP + m], m, late)
        rows = slice(m * PART, (m + 1) * PART)
        total = dot(anom[rows, :], (early if group == 0 else late)[...]) * (1.0 / TIME)
        for i in range(GROUP):
            done[slot, i] = total[:, i * COLW : (i + 1) * COLW]
        copy = pltpu.make_async_copy(done.at[slot], out.at[group * GROUP : (group + 1) * GROUP, rows], sems.at[slot])
        copy.start()
        copies.append(copy)
    for copy in copies[-SLOTS:]:
        copy.wait()


def covariance(at, bp, lagv):
    return pl.pallas_call(
        cov_kernel,
        out_shape=jax.ShapeDtypeStruct((NLAG, ROWW, COLW), F32),
        in_specs=[VMEM] * 3,
        out_specs=HBM,
        scratch_shapes=[
            pltpu.VMEM((ROWW, TIME), BF16),
            pltpu.VMEM((2 * DAYS, TIME), BF16),
            pltpu.VMEM((TIME, 2 * DAYS), BF16),
            pltpu.VMEM((3, TIME + 2 * PAD, 128), F32),
            pltpu.VMEM((TIME, GROUP * COLW), BF16),
            pltpu.VMEM((TIME, GROUP * COLW), BF16),
            pltpu.VMEM((SLOTS, GROUP, PART, COLW), F32),
            DMA((SLOTS,)),
        ],
        compiler_params=pltpu.CompilerParams(vmem_limit_bytes=48 * 2**20),
        name="lagged_covariance",
    )(lagv, at, bp)


def shards(series, day_index, lags):
    return covariance(*gather(series, day_index, lags))


def solution(mesh):
    placed = (P(("row", "col"), None), P(("row", "col")), P())
    return jax.shard_map(
        shards, mesh=mesh, in_specs=placed, out_specs=P(None, "row", "col"), check_vma=False
    )
```

```python
import math

import jax
import jax.numpy as jnp
from jax import lax
from jax.experimental import pallas as pl
from jax.experimental.pallas import tpu as pltpu
from jax.sharding import PartitionSpec as P

NLAG = 8
DAYS = 384
TIME = 2048
NROW = 8
NCOL = 16
STEPS = 16
ROWW = 768
COLW = 384
EXT = ROWW + 16
PAD = 32
CHANS = 6144
GROUP = 4
NPART = 2
PART = ROWW // NPART
SLOTS = 3
MESH = pl.DeviceIdType.MESH
F32 = jnp.float32
BF16 = jnp.bfloat16


class Ring:
    def __init__(self, view, half, slot, device, p, q, send, recv):
        self.view, self.half, self.slot, self.device = view, half, slot, device
        self.p, self.q, self.send, self.recv = p, q, send, recv
        self.copies = {}

    def at(self, dq):
        return lax.rem(self.q + dq + 4, 4)

    def copy(self, n, ref, dev):
        copy = pltpu.make_async_remote_copy(
            src_ref=ref,
            dst_ref=ref,
            send_sem=self.send.at[n],
            recv_sem=self.recv.at[n],
            device_id=dev,
            device_id_type=MESH,
        )
        copy.start()
        self.copies[n] = copy

    def own(self):
        ref = self.view(self.slot(self.p, self.q))
        self.copy(1, ref, self.device(self.p, self.at(1)))
        self.copy(2, ref, self.device(self.p, self.at(-1)))
        self.copy(0, ref, self.device(1 - self.p, self.q))

    def other(self):
        self.copies[0].wait_recv()
        ref = self.view(self.slot(1 - self.p, self.q))
        self.copy(3, ref, self.device(self.p, self.at(1)))
        self.copy(4, ref, self.device(self.p, self.at(-1)))

    def forward(self, n):
        self.copies[n].wait_recv()
        pair = self.p if n < 3 else 1 - self.p
        if n % 2 == 1:
            ref = self.half(self.slot(pair, self.at(-1)), 0)
            self.copy(n + 4, ref, self.device(self.p, self.at(1)))
        else:
            ref = self.half(self.slot(pair, self.at(1)), 1)
            self.copy(n + 4, ref, self.device(self.p, self.at(-1)))


def gather_kernel(
    series, days, lags, at, bp, lagv,
    held, held_days, held_lags, stage, land, sl, sa, ra, sb, rb, sra, rra, srb, rrb, ssib, rsib,
):
    r = lax.axis_index("row")
    c = lax.axis_index("col")
    loads = [
        pltpu.make_async_copy(series, held, sl.at[0]),
        pltpu.make_async_copy(days, held_days, sl.at[1]),
        pltpu.make_async_copy(lags, held_lags, sl.at[2]),
    ]
    for load in loads:
        load.start()
    barrier = pltpu.get_barrier_semaphore()
    for j in range(1, NROW):
        pl.semaphore_signal(barrier, inc=1, device_id=(lax.rem(r + j, NROW), c), device_id_type=MESH)
    for j in range(1, NCOL):
        pl.semaphore_signal(barrier, inc=1, device_id=(r, lax.rem(c + j, NCOL)), device_id_type=MESH)

    for load in loads:
        load.wait()
    step = lax.broadcasted_iota(jnp.int32, (STEPS, 128), 0)
    lane = lax.broadcasted_iota(jnp.int32, (STEPS, 128), 1)
    day = jnp.zeros((STEPS, 128), jnp.int32)
    for i in range(STEPS):
        day = jnp.where(step == i, held_days[i], day)
    high = jnp.right_shift(day, 8)
    info = jnp.where(lane == 0, high, jnp.where(lane == 1, day - high * 256, 0))
    info = info.astype(F32).astype(BF16)
    for d in range(NROW):
        stage[d, :, :ROWW] = held[:, d * ROWW : (d + 1) * ROWW]
        stage[d, :, ROWW:] = info

    for k in range(NLAG):
        lagv[k : k + 1, :] = jnp.full((1, 128), held_lags[k], jnp.int32).astype(F32)
    pl.semaphore_wait(barrier, NROW + NCOL - 2)

    rows, cols = [], []
    for j in range(1, NROW):
        to = lax.rem(r + j, NROW)
        copy = pltpu.make_async_remote_copy(
            src_ref=stage.at[to],
            dst_ref=land.at[r],
            send_sem=sa.at[j],
            recv_sem=ra.at[j],
            device_id=(to, c),
            device_id_type=MESH,
        )
        copy.start()
        rows.append(copy)
    for j in range(1, NCOL):
        to = lax.rem(c + j, NCOL)
        copy = pltpu.make_async_remote_copy(
            src_ref=held.at[:, pl.ds(pl.multiple_of(to * COLW, 128), COLW)],
            dst_ref=bp.at[c, r],
            send_sem=sb.at[j],
            recv_sem=rb.at[j],
            device_id=(r, to),
            device_id_type=MESH,
        )
        copy.start()
        cols.append(copy)
    land[r] = stage[r]
    bp[c, r] = held[:, pl.ds(pl.multiple_of(c * COLW, 128), COLW)]

    core = lax.rem(c, 2)
    ring_a = Ring(
        lambda s: at.at[s],
        lambda s, h: at.at[s, 400 * h : 400 + 384 * h],
        lambda p, q: p * 8 + q * 2 + core,
        lambda p, q: (r, p * 8 + q * 2 + core),
        c // 8,
        lax.rem(c // 2, 4),
        sra,
        rra,
    )
    ring_b = Ring(
        lambda s: bp.at[:, s],
        lambda s, h: bp.at[8 * h : 8 * h + 8, s],
        lambda p, q: p * 4 + q,
        lambda p, q: (p * 4 + q, c),
        r // 4,
        lax.rem(r, 4),
        srb,
        rrb,
    )
    siblings = []

    def sibling(p, q):
        n = len(siblings)
        ref = at.at[ring_a.slot(p, q)]
        copy = pltpu.make_async_remote_copy(
            src_ref=ref,
            dst_ref=ref,
            send_sem=ssib.at[n],
            recv_sem=rsib.at[n],
            device_id=(r, c + 1 - 2 * core),
            device_id_type=MESH,
        )
        copy.start()
        siblings.append(copy)

    for copy in rows:
        copy.wait_recv()
    block = land[...].reshape(NROW * STEPS, ROWW + 128).astype(F32)
    at[c] = block.T[:EXT].astype(BF16)
    ring_a.own()
    for copy in cols:
        copy.wait_recv()
    ring_b.own()
    pa, qa = ring_a.p, ring_a.q
    sibling(pa, qa)
    ring_a.other()
    ring_b.other()
    ring_a.forward(1)
    ring_a.forward(2)
    ring_b.forward(1)
    ring_b.forward(2)
    sibling(1 - pa, qa)
    sibling(pa, ring_a.at(-1))
    sibling(pa, ring_a.at(1))
    ring_a.forward(3)
    ring_a.forward(4)
    ring_b.forward(3)
    ring_b.forward(4)
    sibling(1 - pa, ring_a.at(-1))
    sibling(1 - pa, ring_a.at(1))
    for pair, first in ((pa, 5), (1 - pa, 7)):
        ring_a.copies[first].wait_recv()
        ring_a.copies[first + 1].wait_recv()
        sibling(pair, ring_a.at(2))
    for n in (5, 6, 7, 8):
        ring_b.copies[n].wait_recv()
    for copy in siblings:
        copy.wait()
    for copy in rows + cols + list(ring_a.copies.values()) + list(ring_b.copies.values()):
        copy.wait_send()


def hbm(x):
    return pltpu.with_memory_space_constraint(x, pltpu.HBM)


HBM = pl.BlockSpec(memory_space=pltpu.HBM)
VMEM = pl.BlockSpec(memory_space=pltpu.VMEM)
DMA = pltpu.SemaphoreType.DMA


def gather(series, day_index, lags):
    return pl.pallas_call(
        gather_kernel,
        out_shape=(
            jax.ShapeDtypeStruct((NCOL, EXT, 128), BF16),
            jax.ShapeDtypeStruct((NCOL, NROW, STEPS, COLW), BF16),
            jax.ShapeDtypeStruct((NLAG, 128), F32),
        ),
        in_specs=[HBM, HBM, HBM],
        out_specs=(VMEM, VMEM, VMEM),
        scratch_shapes=[
            pltpu.VMEM((STEPS, CHANS), BF16),
            pltpu.SMEM((STEPS,), jnp.int32),
            pltpu.SMEM((NLAG,), jnp.int32),
            pltpu.VMEM((NROW, STEPS, ROWW + 128), BF16),
            pltpu.VMEM((NROW, STEPS, ROWW + 128), BF16),
            DMA((3,)),
            DMA((NROW,)),
            DMA((NROW,)),
            DMA((NCOL,)),
            DMA((NCOL,)),
            DMA((9,)),
            DMA((9,)),
            DMA((9,)),
            DMA((9,)),
            DMA((8,)),
            DMA((8,)),
        ],
        compiler_params=pltpu.CompilerParams(
            collective_id=0, has_side_effects=True, vmem_limit_bytes=8 * 2**20
        ),
        name="gather_series",
    )(hbm(series), hbm(day_index), hbm(lags))


def fill(pad, lag, i, held):
    for k in range(NCOL):
        for b in range(NROW):
            to = (k * NROW + b) * 16
            for w in range(3):
                piece = pad[w, pl.ds(PAD + b * 256 + k * 16 + lag, 16), :]
                held[to : to + 16, i * COLW + w * 128 : i * COLW + (w + 1) * 128] = piece.astype(BF16)


def dot(a, b):
    return jnp.dot(a, b, preferred_element_type=F32)


def split(x):
    high = x.astype(BF16)
    return high, (x - high.astype(F32)).astype(BF16)


def cov_kernel(lagv, at, bp, out, anom, onehot, onehot_t, pad, early, late, done, sems):
    lag = [jnp.max(lagv[k : k + 1, :]).astype(jnp.int32) for k in range(NLAG)]
    place = lax.broadcasted_iota(jnp.int32, (NCOL, 128), 1)
    when = place // STEPS * (NCOL * STEPS) + lax.broadcasted_iota(jnp.int32, (NCOL, 128), 0) * STEPS + place % STEPS
    taper = 0.5 - 0.5 * jnp.cos(2.0 * math.pi * (when.astype(F32) + 0.5) / TIME)
    taper_t = taper.T

    info = at[:, ROWW:, :].astype(F32)
    day = info[:, 0, :] * 256.0 + info[:, 1, :]
    day_t = day.T
    down = lax.broadcasted_iota(jnp.int32, (DAYS, 128), 0).astype(F32)
    along = lax.broadcasted_iota(jnp.int32, (128, DAYS), 1).astype(F32)
    count = jnp.zeros((DAYS, 128), F32)
    for k in range(NCOL):
        steps = slice(k * 128, (k + 1) * 128)
        anom[:, steps] = at[k, :ROWW, :]
        here = jnp.where(down == day[k : k + 1, :], 1.0, 0.0)
        count = count + here
        hot = here.astype(BF16)
        onehot[:DAYS, steps] = hot
        onehot[DAYS:, steps] = hot
        hot = jnp.where(along == day_t[:, k : k + 1], 1.0, 0.0).astype(BF16)
        onehot_t[steps, :DAYS] = hot
        onehot_t[steps, DAYS:] = hot
    inv_col = 1.0 / jnp.maximum(jnp.sum(count, axis=1, keepdims=True), 1.0)
    inv_row = jnp.broadcast_to(inv_col, (DAYS, 128)).T[0:1, :]

    sums = dot(onehot[:DAYS, :], bp[...].reshape(TIME, COLW))
    both = jnp.concatenate(split(sums * inv_col), axis=0)
    pad[:, :PAD, :] = jnp.zeros((3, PAD, 128), F32)
    pad[:, PAD + TIME :, :] = jnp.zeros((3, PAD, 128), F32)
    for q in range(4):
        season = dot(onehot_t[q * 512 : (q + 1) * 512, :], both)
        for k in range(4 * q, 4 * q + 4):
            here = bp[k].reshape(128, COLW).astype(F32) - season[(k - 4 * q) * 128 : (k - 4 * q + 1) * 128]
            here = (here * taper_t[:, k : k + 1]).astype(BF16).astype(F32)
            for b in range(NROW):
                row = PAD + b * 256 + k * 16
                for w in range(3):
                    pad[w, row : row + 16, :] = here[b * 16 : (b + 1) * 16, w * 128 : (w + 1) * 128]

    sums = lax.dot_general(anom[...], onehot[:DAYS, :], (((1,), (1,)), ((), ())), preferred_element_type=F32)
    both = jnp.concatenate(split(sums * inv_row), axis=1)
    for n in range(4):
        fill(pad, lag[n], n, early)
        season = dot(both, onehot[:, n * 512 : (n + 1) * 512])
        for k in range(4 * n, 4 * n + 4):
            steps = slice(k * 128, (k + 1) * 128)
            here = anom[:, steps].astype(F32) - season[:, (k - 4 * n) * 128 : (k - 4 * n + 1) * 128]
            anom[:, steps] = (here * taper[k : k + 1, :]).astype(BF16)

    copies = []
    for n in range(2 * NPART):
        group, m = divmod(n, NPART)
        slot = n % SLOTS
        if n >= SLOTS:
            copies[n - SLOTS].wait()
        if group == 0:
            for k in range(m * GROUP // NPART, (m + 1) * GROUP // NPART):
                fill(pad, lag[GROUP + k], k, late)
        rows = slice(m * PART, (m + 1) * PART)
        total = dot(anom[rows, :], (early if group == 0 else late)[...]) * (1.0 / TIME)
        for i in range(GROUP):
            done[slot, i] = total[:, i * COLW : (i + 1) * COLW]
        copy = pltpu.make_async_copy(done.at[slot], out.at[group * GROUP : (group + 1) * GROUP, rows], sems.at[slot])
        copy.start()
        copies.append(copy)
    for copy in copies[-SLOTS:]:
        copy.wait()


def covariance(at, bp, lagv):
    return pl.pallas_call(
        cov_kernel,
        out_shape=jax.ShapeDtypeStruct((NLAG, ROWW, COLW), F32),
        in_specs=[VMEM] * 3,
        out_specs=HBM,
        scratch_shapes=[
            pltpu.VMEM((ROWW, TIME), BF16),
            pltpu.VMEM((2 * DAYS, TIME), BF16),
            pltpu.VMEM((TIME, 2 * DAYS), BF16),
            pltpu.VMEM((3, TIME + 2 * PAD, 128), F32),
            pltpu.VMEM((TIME, GROUP * COLW), BF16),
            pltpu.VMEM((TIME, GROUP * COLW), BF16),
            pltpu.VMEM((SLOTS, GROUP, PART, COLW), F32),
            DMA((SLOTS,)),
        ],
        compiler_params=pltpu.CompilerParams(vmem_limit_bytes=48 * 2**20),
        name="lagged_covariance",
    )(lagv, at, bp)


def shards(series, day_index, lags):
    return covariance(*gather(series, day_index, lags))


def solution(mesh):
    placed = (P(("row", "col"), None), P(("row", "col")), P())
    return jax.shard_map(
        shards, mesh=mesh, in_specs=placed, out_specs=P(None, "row", "col"), check_vma=False
    )
```

```python
import math

import jax
import jax.numpy as jnp
from jax import lax
from jax.experimental import pallas as pl
from jax.experimental.pallas import tpu as pltpu
from jax.sharding import PartitionSpec as P

NLAG = 8
DAYS = 384
TIME = 2048
NROW = 8
NCOL = 16
STEPS = 16
ROWW = 768
COLW = 384
EXT = ROWW + 16
PAD = 32
INFO = 16
HALF = ROWW // 2
COLS = (0, 256, 384)
ROWS = (0, INFO + HALF, EXT)
MIDS = (208, 592)
CHANS = 6144
GROUP = 4
SLOTS = 2
MESH = pl.DeviceIdType.MESH
F32 = jnp.float32
BF16 = jnp.bfloat16


class Ring:
    def __init__(self, view, half, slot, device, p, q, send, recv):
        self.view, self.half, self.slot, self.device = view, half, slot, device
        self.p, self.q, self.send, self.recv = p, q, send, recv
        self.copies = {}

    def at(self, dq):
        return lax.rem(self.q + dq + 4, 4)

    def copy(self, j, n, ref, dev):
        copy = pltpu.make_async_remote_copy(
            src_ref=ref,
            dst_ref=ref,
            send_sem=self.send.at[j, n],
            recv_sem=self.recv.at[j, n],
            device_id=dev,
            device_id_type=MESH,
        )
        copy.start()
        self.copies[j, n] = copy

    def own(self, j):
        ref = self.view(self.slot(self.p, self.q), j)
        self.copy(j, 0, ref, self.device(1 - self.p, self.q))
        self.copy(j, 1, ref, self.device(self.p, self.at(1)))
        self.copy(j, 2, ref, self.device(self.p, self.at(-1)))

    def other(self, j):
        self.copies[j, 0].wait_recv()
        ref = self.view(self.slot(1 - self.p, self.q), j)
        self.copy(j, 3, ref, self.device(self.p, self.at(1)))
        self.copy(j, 4, ref, self.device(self.p, self.at(-1)))

    def forward(self, j, n):
        self.copies[j, n].wait_recv()
        pair = self.p if n < 3 else 1 - self.p
        if n % 2 == 1:
            self.copy(j, n + 4, self.half(self.slot(pair, self.at(-1)), j, 0), self.device(self.p, self.at(1)))
        else:
            self.copy(j, n + 4, self.half(self.slot(pair, self.at(1)), j, 1), self.device(self.p, self.at(-1)))


def dot(a, b):
    return jnp.dot(a, b, preferred_element_type=F32)


def split(x):
    high = x.astype(BF16)
    return high, (x - high.astype(F32)).astype(BF16)


def taper_of():
    place = lax.broadcasted_iota(jnp.int32, (NCOL, 128), 1)
    when = place // STEPS * (NCOL * STEPS) + lax.broadcasted_iota(jnp.int32, (NCOL, 128), 0) * STEPS + place % STEPS
    return 0.5 - 0.5 * jnp.cos(2.0 * math.pi * (when.astype(F32) + 0.5) / TIME)


def column_part(bp, j, onehot, onehot_t, inv_col, taper_t, pad):
    lanes = slice(COLS[j], COLS[j + 1])
    width = COLS[j + 1] - COLS[j]
    sums = dot(onehot[:DAYS, :], bp[:, :, :, lanes].reshape(TIME, width))
    both = jnp.concatenate(split(sums * inv_col), axis=0)
    pad[:, :PAD, :] = jnp.zeros((width // 128, PAD, 128), F32)
    pad[:, PAD + TIME :, :] = jnp.zeros((width // 128, PAD, 128), F32)
    for q in range(4):
        season = dot(onehot_t[q * 512 : (q + 1) * 512, :], both)
        for k in range(4 * q, 4 * q + 4):
            here = bp[k, :, :, lanes].reshape(128, width).astype(F32) - season[(k - 4 * q) * 128 : (k - 4 * q + 1) * 128]
            here = (here * taper_t[:, k : k + 1]).astype(BF16).astype(F32)
            for b in range(NROW):
                row = PAD + b * 256 + k * 16
                for w in range(width // 128):
                    pad[w, row : row + 16, :] = here[b * 16 : (b + 1) * 16, w * 128 : (w + 1) * 128]


def row_sums(at, j, onehot, inv_row, anom):
    first = INFO + j * HALF
    for k in range(NCOL):
        anom[:, k * 128 : (k + 1) * 128] = at[k, first : first + HALF, :]
    sums = lax.dot_general(anom[...], onehot[:DAYS, :], (((1,), (1,)), ((), ())), preferred_element_type=F32)
    return jnp.concatenate(split(sums * inv_row), axis=1)


def row_part(both, n, onehot, taper, anom):
    season = dot(both, onehot[:, n * 512 : (n + 1) * 512])
    for k in range(4 * n, 4 * n + 4):
        steps = slice(k * 128, (k + 1) * 128)
        here = anom[:, steps].astype(F32) - season[:, (k - 4 * n) * 128 : (k - 4 * n + 1) * 128]
        anom[:, steps] = (here * taper[k : k + 1, :]).astype(BF16)


def gather_kernel(
    series, days, lags, at, bp, lagv, onehot, onehot_t, invs, anom, pad,
    held, held_days, held_lags, stage, land, sl, sa, ra, sb, rb, sra, rra, srb, rrb, ssib, rsib,
):
    r = lax.axis_index("row")
    c = lax.axis_index("col")
    loads = [
        pltpu.make_async_copy(series, held, sl.at[0]),
        pltpu.make_async_copy(days, held_days, sl.at[1]),
        pltpu.make_async_copy(lags, held_lags, sl.at[2]),
    ]
    for load in loads:
        load.start()
    barrier = pltpu.get_barrier_semaphore()
    for j in range(1, NROW):
        pl.semaphore_signal(barrier, inc=1, device_id=(lax.rem(r + j, NROW), c), device_id_type=MESH)
    for j in range(1, NCOL):
        pl.semaphore_signal(barrier, inc=1, device_id=(r, lax.rem(c + j, NCOL)), device_id_type=MESH)

    for load in loads:
        load.wait()
    step = lax.broadcasted_iota(jnp.int32, (STEPS, 128), 0)
    lane = lax.broadcasted_iota(jnp.int32, (STEPS, 128), 1)
    day = jnp.zeros((STEPS, 128), jnp.int32)
    for i in range(STEPS):
        day = jnp.where(step == i, held_days[i], day)
    high = jnp.right_shift(day, 8)
    info = jnp.where(lane == 0, high, jnp.where(lane == 1, day - high * 256, 0))
    info = info.astype(F32).astype(BF16)
    for d in range(NROW):
        stage[d, :, :ROWW] = held[:, d * ROWW : (d + 1) * ROWW]
        stage[d, :, ROWW:] = info

    for k in range(NLAG):
        lagv[k : k + 1, :] = jnp.full((1, 128), held_lags[k], jnp.int32).astype(F32)
    pl.semaphore_wait(barrier, NROW + NCOL - 2)

    rows, cols = [], []
    for j in range(1, NROW):
        to = lax.rem(r + j, NROW)
        copy = pltpu.make_async_remote_copy(
            src_ref=stage.at[to],
            dst_ref=land.at[r],
            send_sem=sa.at[j],
            recv_sem=ra.at[j],
            device_id=(to, c),
            device_id_type=MESH,
        )
        copy.start()
        rows.append(copy)
    for j in range(1, NCOL):
        to = lax.rem(c + j, NCOL)
        copy = pltpu.make_async_remote_copy(
            src_ref=held.at[:, pl.ds(pl.multiple_of(to * COLW, 128), COLW)],
            dst_ref=bp.at[c, r],
            send_sem=sb.at[j],
            recv_sem=rb.at[j],
            device_id=(r, to),
            device_id_type=MESH,
        )
        copy.start()
        cols.append(copy)
    land[r] = stage[r]
    bp[c, r] = held[:, pl.ds(pl.multiple_of(c * COLW, 128), COLW)]

    core = lax.rem(c, 2)
    ring_a = Ring(
        lambda s, j: at.at[s, ROWS[j] : ROWS[j + 1]],
        lambda s, j, h: at.at[s, (ROWS[j], MIDS[j])[h] : (MIDS[j], ROWS[j + 1])[h]],
        lambda p, q: p * 8 + q * 2 + core,
        lambda p, q: (r, p * 8 + q * 2 + core),
        c // 8,
        lax.rem(c // 2, 4),
        sra,
        rra,
    )
    ring_b = Ring(
        lambda s, j: bp.at[:, s, :, COLS[j] : COLS[j + 1]],
        lambda s, j, h: bp.at[8 * h : 8 * h + 8, s, :, COLS[j] : COLS[j + 1]],
        lambda p, q: p * 4 + q,
        lambda p, q: (p * 4 + q, c),
        r // 4,
        lax.rem(r, 4),
        srb,
        rrb,
    )
    pa, qa = ring_a.p, ring_a.q
    siblings = {}

    def sibling(j, p, q):
        n = sum(key[0] == j for key in siblings)
        ref = ring_a.view(ring_a.slot(p, q), j)
        copy = pltpu.make_async_remote_copy(
            src_ref=ref,
            dst_ref=ref,
            send_sem=ssib.at[j, n],
            recv_sem=rsib.at[j, n],
            device_id=(r, c + 1 - 2 * core),
            device_id_type=MESH,
        )
        copy.start()
        siblings[j, n] = copy

    def other(j):
        ring_a.other(j)
        ring_b.other(j)

    def near(j):
        for n in (1, 2):
            ring_a.forward(j, n)
            ring_b.forward(j, n)

    def far(j):
        for n in (3, 4):
            ring_a.forward(j, n)
            ring_b.forward(j, n)

    def last(j):
        for n, p in ((5, pa), (7, 1 - pa)):
            ring_a.copies[j, n].wait_recv()
            ring_a.copies[j, n + 1].wait_recv()
            sibling(j, p, ring_a.at(2))
        for n in (5, 6, 7, 8):
            ring_b.copies[j, n].wait_recv()

    for copy in rows:
        copy.wait_recv()
    block = land[...].reshape(NROW * STEPS, ROWW + 128).astype(F32).T
    at[c, :INFO] = block[ROWW:EXT].astype(BF16)
    at[c, INFO:] = block[:ROWW].astype(BF16)
    ring_a.own(0)
    for copy in cols:
        copy.wait_recv()
    ring_b.own(0)
    sibling(0, pa, qa)
    taper = taper_of()
    taper_t = taper.T
    other(0)
    near(0)
    ring_a.own(1)
    ring_b.own(1)
    sibling(0, 1 - pa, qa)
    sibling(0, pa, ring_a.at(-1))
    sibling(0, pa, ring_a.at(1))
    far(0)
    sibling(0, 1 - pa, ring_a.at(-1))
    sibling(0, 1 - pa, ring_a.at(1))
    sibling(1, pa, qa)
    other(1)
    last(0)
    near(1)
    sibling(1, 1 - pa, qa)
    sibling(1, pa, ring_a.at(-1))
    sibling(1, pa, ring_a.at(1))
    for n in range(8):
        siblings[0, n].wait_recv()

    info = at[:, :INFO, :].astype(F32)
    day = info[:, 0, :] * 256.0 + info[:, 1, :]
    day_t = day.T
    down = lax.broadcasted_iota(jnp.int32, (DAYS, 128), 0).astype(F32)
    along = lax.broadcasted_iota(jnp.int32, (128, DAYS), 1).astype(F32)
    count = jnp.zeros((DAYS, 128), F32)
    for k in range(NCOL):
        steps = slice(k * 128, (k + 1) * 128)
        here = jnp.where(down == day[k : k + 1, :], 1.0, 0.0)
        count = count + here
        hot = here.astype(BF16)
        onehot[:DAYS, steps] = hot
        onehot[DAYS:, steps] = hot
        hot = jnp.where(along == day_t[:, k : k + 1], 1.0, 0.0).astype(BF16)
        onehot_t[steps, :DAYS] = hot
        onehot_t[steps, DAYS:] = hot
    inv = 1.0 / jnp.maximum(jnp.sum(count, axis=1, keepdims=True), 1.0)
    invs[...] = jnp.broadcast_to(inv, (DAYS, 128))
    inv_row = invs[...].T[0:1, :]
    far(1)
    sibling(1, 1 - pa, ring_a.at(-1))
    sibling(1, 1 - pa, ring_a.at(1))
    column_part(bp, 0, onehot, onehot_t, inv, taper_t, pad)
    both = row_sums(at, 0, onehot, inv_row, anom)
    last(1)
    for n in range(4):
        row_part(both, n, onehot, taper, anom)
    for n in range(8):
        siblings[1, n].wait_recv()
    for copy in rows + cols + list(siblings.values()) + list(ring_a.copies.values()) + list(ring_b.copies.values()):
        copy.wait_send()


def hbm(x):
    return pltpu.with_memory_space_constraint(x, pltpu.HBM)


HBM = pl.BlockSpec(memory_space=pltpu.HBM)
VMEM = pl.BlockSpec(memory_space=pltpu.VMEM)
DMA = pltpu.SemaphoreType.DMA


def gather(series, day_index, lags):
    return pl.pallas_call(
        gather_kernel,
        out_shape=(
            jax.ShapeDtypeStruct((NCOL, EXT, 128), BF16),
            jax.ShapeDtypeStruct((NCOL, NROW, STEPS, COLW), BF16),
            jax.ShapeDtypeStruct((NLAG, 128), F32),
            jax.ShapeDtypeStruct((2 * DAYS, TIME), BF16),
            jax.ShapeDtypeStruct((TIME, 2 * DAYS), BF16),
            jax.ShapeDtypeStruct((DAYS, 128), F32),
            jax.ShapeDtypeStruct((HALF, TIME), BF16),
            jax.ShapeDtypeStruct((2, TIME + 2 * PAD, 128), F32),
        ),
        in_specs=[HBM, HBM, HBM],
        out_specs=(VMEM,) * 8,
        scratch_shapes=[
            pltpu.VMEM((STEPS, CHANS), BF16),
            pltpu.SMEM((STEPS,), jnp.int32),
            pltpu.SMEM((NLAG,), jnp.int32),
            pltpu.VMEM((NROW, STEPS, ROWW + 128), BF16),
            pltpu.VMEM((NROW, STEPS, ROWW + 128), BF16),
            DMA((3,)),
            DMA((NROW,)),
            DMA((NROW,)),
            DMA((NCOL,)),
            DMA((NCOL,)),
            DMA((2, 9)),
            DMA((2, 9)),
            DMA((2, 9)),
            DMA((2, 9)),
            DMA((2, 8)),
            DMA((2, 8)),
        ],
        compiler_params=pltpu.CompilerParams(
            collective_id=0, has_side_effects=True, vmem_limit_bytes=12 * 2**20
        ),
        name="gather_series",
    )(hbm(series), hbm(day_index), hbm(lags))


def fill(pads, lag, i, held):
    for k in range(NCOL):
        for b in range(NROW):
            to = (k * NROW + b) * 16
            for w in range(3):
                piece = pads[w // 2][w % 2, pl.ds(PAD + b * 256 + k * 16 + lag, 16), :]
                held[to : to + 16, i * COLW + w * 128 : i * COLW + (w + 1) * 128] = piece.astype(BF16)


def cov_kernel(at, bp, lagv, onehot, onehot_t, invs, anom0, pad0, out, anom1, pad1, early, late, done, sems):
    lag = [jnp.max(lagv[k : k + 1, :]).astype(jnp.int32) for k in range(NLAG)]
    taper = taper_of()
    column_part(bp, 1, onehot, onehot_t, invs[:, 0:1], taper.T, pad1)
    both = row_sums(at, 1, onehot, invs[...].T[0:1, :], anom1)
    pads = (pad0, pad1)
    for n in range(4):
        fill(pads, lag[n], n, early)
        row_part(both, n, onehot, taper, anom1)

    copies = []
    for n in range(4):
        group, m = divmod(n, 2)
        slot = n % SLOTS
        if n >= SLOTS:
            copies[n - SLOTS].wait()
        if group == 0:
            for k in range(2 * m, 2 * m + 2):
                fill(pads, lag[GROUP + k], k, late)
        total = dot((anom0, anom1)[m][...], (early, late)[group][...]) * (1.0 / TIME)
        for i in range(GROUP):
            done[slot, i] = total[:, i * COLW : (i + 1) * COLW]
        copy = pltpu.make_async_copy(
            done.at[slot],
            out.at[group * GROUP : (group + 1) * GROUP, m * HALF : (m + 1) * HALF],
            sems.at[slot],
        )
        copy.start()
        copies.append(copy)
    for copy in copies[-SLOTS:]:
        copy.wait()


def covariance(*gathered):
    return pl.pallas_call(
        cov_kernel,
        out_shape=jax.ShapeDtypeStruct((NLAG, ROWW, COLW), F32),
        in_specs=[VMEM] * 8,
        out_specs=HBM,
        scratch_shapes=[
            pltpu.VMEM((HALF, TIME), BF16),
            pltpu.VMEM((1, TIME + 2 * PAD, 128), F32),
            pltpu.VMEM((TIME, GROUP * COLW), BF16),
            pltpu.VMEM((TIME, GROUP * COLW), BF16),
            pltpu.VMEM((SLOTS, GROUP, HALF, COLW), F32),
            DMA((SLOTS,)),
        ],
        compiler_params=pltpu.CompilerParams(vmem_limit_bytes=30 * 2**20),
        name="lagged_covariance",
    )(*gathered)


def shards(series, day_index, lags):
    return covariance(*gather(series, day_index, lags))


def solution(mesh):
    placed = (P(("row", "col"), None), P(("row", "col")), P())
    return jax.shard_map(
        shards, mesh=mesh, in_specs=placed, out_specs=P(None, "row", "col"), check_vma=False
    )
```

```python
import math

import jax
import jax.numpy as jnp
from jax import lax
from jax.experimental import pallas as pl
from jax.experimental.pallas import tpu as pltpu
from jax.sharding import PartitionSpec as P

NLAG = 8
DAYS = 384
TIME = 2048
NROW = 8
NCOL = 16
STEPS = 16
ROWW = 768
COLW = 384
EXT = ROWW + 16
PAD = 32
CHANS = 6144
GROUP = 4
NPART = 2
PART = ROWW // NPART
SLOTS = 2
MESH = pl.DeviceIdType.MESH
F32 = jnp.float32
BF16 = jnp.bfloat16


class Ring:
    def __init__(self, view, half, slot, device, p, q, send, recv):
        self.view, self.half, self.slot, self.device = view, half, slot, device
        self.p, self.q, self.send, self.recv = p, q, send, recv
        self.copies = {}

    def at(self, dq):
        return lax.rem(self.q + dq + 4, 4)

    def copy(self, n, ref, dev):
        copy = pltpu.make_async_remote_copy(
            src_ref=ref,
            dst_ref=ref,
            send_sem=self.send.at[n],
            recv_sem=self.recv.at[n],
            device_id=dev,
            device_id_type=MESH,
        )
        copy.start()
        self.copies[n] = copy

    def own(self):
        ref = self.view(self.slot(self.p, self.q))
        self.copy(0, ref, self.device(1 - self.p, self.q))
        self.copy(1, ref, self.device(self.p, self.at(1)))
        self.copy(2, ref, self.device(self.p, self.at(-1)))

    def other(self):
        self.copies[0].wait_recv()
        ref = self.view(self.slot(1 - self.p, self.q))
        self.copy(3, ref, self.device(self.p, self.at(1)))
        self.copy(4, ref, self.device(self.p, self.at(-1)))

    def forward(self, n):
        self.copies[n].wait_recv()
        pair = self.p if n < 3 else 1 - self.p
        if n % 2 == 1:
            ref = self.half(self.slot(pair, self.at(-1)), 0)
            self.copy(n + 4, ref, self.device(self.p, self.at(1)))
        else:
            ref = self.half(self.slot(pair, self.at(1)), 1)
            self.copy(n + 4, ref, self.device(self.p, self.at(-1)))


def gather_kernel(
    series, days, lags, at, bp, lagv, onehot, onehot_t, invs, taper, taper_t,
    count, held, held_days, held_lags, stage, land, sl, sa, ra, sb, rb, sra, rra, srb, rrb, ssib, rsib,
):
    r = lax.axis_index("row")
    c = lax.axis_index("col")
    loads = [
        pltpu.make_async_copy(series, held, sl.at[0]),
        pltpu.make_async_copy(days, held_days, sl.at[1]),
        pltpu.make_async_copy(lags, held_lags, sl.at[2]),
    ]
    for load in loads:
        load.start()
    barrier = pltpu.get_barrier_semaphore()
    for j in range(1, NROW):
        pl.semaphore_signal(barrier, inc=1, device_id=(lax.rem(r + j, NROW), c), device_id_type=MESH)
    for j in range(1, NCOL):
        pl.semaphore_signal(barrier, inc=1, device_id=(r, lax.rem(c + j, NCOL)), device_id_type=MESH)

    for load in loads:
        load.wait()
    step = lax.broadcasted_iota(jnp.int32, (STEPS, 128), 0)
    lane = lax.broadcasted_iota(jnp.int32, (STEPS, 128), 1)
    day = jnp.zeros((STEPS, 128), jnp.int32)
    for i in range(STEPS):
        day = jnp.where(step == i, held_days[i], day)
    high = jnp.right_shift(day, 8)
    info = jnp.where(lane == 0, high, jnp.where(lane == 1, day - high * 256, 0))
    info = info.astype(F32).astype(BF16)
    for d in range(NROW):
        stage[d, :, :ROWW] = held[:, d * ROWW : (d + 1) * ROWW]
        stage[d, :, ROWW:] = info

    for k in range(NLAG):
        lagv[k : k + 1, :] = jnp.full((1, 128), held_lags[k], jnp.int32).astype(F32)
    pl.semaphore_wait(barrier, NROW + NCOL - 2)

    rows, cols = [], []
    for j in range(1, NROW):
        to = lax.rem(r + j, NROW)
        copy = pltpu.make_async_remote_copy(
            src_ref=stage.at[to],
            dst_ref=land.at[r],
            send_sem=sa.at[j],
            recv_sem=ra.at[j],
            device_id=(to, c),
            device_id_type=MESH,
        )
        copy.start()
        rows.append(copy)
    for j in range(1, NCOL):
        to = lax.rem(c + j, NCOL)
        copy = pltpu.make_async_remote_copy(
            src_ref=held.at[:, pl.ds(pl.multiple_of(to * COLW, 128), COLW)],
            dst_ref=bp.at[c, r],
            send_sem=sb.at[j],
            recv_sem=rb.at[j],
            device_id=(r, to),
            device_id_type=MESH,
        )
        copy.start()
        cols.append(copy)
    land[r] = stage[r]
    bp[c, r] = held[:, pl.ds(pl.multiple_of(c * COLW, 128), COLW)]

    core = lax.rem(c, 2)
    ring_a = Ring(
        lambda s: at.at[s],
        lambda s, h: at.at[s, 400 * h : 400 + 384 * h],
        lambda p, q: p * 8 + q * 2 + core,
        lambda p, q: (r, p * 8 + q * 2 + core),
        c // 8,
        lax.rem(c // 2, 4),
        sra,
        rra,
    )
    ring_b = Ring(
        lambda s: bp.at[:, s],
        lambda s, h: bp.at[8 * h : 8 * h + 8, s],
        lambda p, q: p * 4 + q,
        lambda p, q: (p * 4 + q, c),
        r // 4,
        lax.rem(r, 4),
        srb,
        rrb,
    )
    siblings = []

    def sibling(p, q):
        n = len(siblings)
        ref = at.at[ring_a.slot(p, q)]
        copy = pltpu.make_async_remote_copy(
            src_ref=ref,
            dst_ref=ref,
            send_sem=ssib.at[n],
            recv_sem=rsib.at[n],
            device_id=(r, c + 1 - 2 * core),
            device_id_type=MESH,
        )
        copy.start()
        siblings.append(copy)

    down = lax.broadcasted_iota(jnp.int32, (DAYS, 128), 0).astype(F32)
    along = lax.broadcasted_iota(jnp.int32, (128, DAYS), 1).astype(F32)

    def hot(slot):
        info = at[slot, ROWW:, :].astype(F32)
        day = info[0:1] * 256.0 + info[1:2]
        steps = pl.ds(pl.multiple_of(slot * 128, 128), 128)
        here = jnp.where(down == day, 1.0, 0.0)
        count[...] += here
        here = here.astype(BF16)
        onehot[:DAYS, steps] = here
        onehot[DAYS:, steps] = here
        day_t = jnp.broadcast_to(day, (128, 128)).T[:, 0:1]
        here = jnp.where(along == day_t, 1.0, 0.0).astype(BF16)
        onehot_t[steps, :DAYS] = here
        onehot_t[steps, DAYS:] = here

    def hot_sibling(n, p, q):
        siblings[n].wait_recv()
        hot(p * 8 + q * 2 + 1 - core)

    for copy in rows:
        copy.wait_recv()
    block = land[...].reshape(NROW * STEPS, ROWW + 128).astype(F32)
    at[c] = block.T[:EXT].astype(BF16)
    ring_a.own()
    for copy in cols:
        copy.wait_recv()
    ring_b.own()
    pa, qa = ring_a.p, ring_a.q
    po = 1 - pa
    down_q, up_q, far_q = ring_a.at(-1), ring_a.at(1), ring_a.at(2)
    sibling(pa, qa)
    place = lax.broadcasted_iota(jnp.int32, (NCOL, 128), 1)
    when = place // STEPS * (NCOL * STEPS) + lax.broadcasted_iota(jnp.int32, (NCOL, 128), 0) * STEPS + place % STEPS
    wave = 0.5 - 0.5 * jnp.cos(2.0 * math.pi * (when.astype(F32) + 0.5) / TIME)
    taper[...] = wave
    taper_t[...] = wave.T
    count[...] = jnp.zeros((DAYS, 128), F32)
    hot(c)
    ring_a.other()
    ring_b.other()
    for n in (1, 2):
        ring_a.forward(n)
        ring_b.forward(n)
    sibling(po, qa)
    sibling(pa, down_q)
    sibling(pa, up_q)
    hot(ring_a.slot(po, qa))
    hot(ring_a.slot(pa, down_q))
    hot(ring_a.slot(pa, up_q))
    hot_sibling(0, pa, qa)
    for n in (3, 4):
        ring_a.forward(n)
        ring_b.forward(n)
    sibling(po, down_q)
    sibling(po, up_q)
    hot(ring_a.slot(po, down_q))
    hot(ring_a.slot(po, up_q))
    for n in (5, 6):
        ring_a.copies[n].wait_recv()
    sibling(pa, far_q)
    hot(ring_a.slot(pa, far_q))
    hot_sibling(1, po, qa)
    hot_sibling(2, pa, down_q)
    hot_sibling(3, pa, up_q)
    for n in (7, 8):
        ring_a.copies[n].wait_recv()
    sibling(po, far_q)
    hot(ring_a.slot(po, far_q))
    hot_sibling(4, po, down_q)
    hot_sibling(5, po, up_q)
    hot_sibling(6, pa, far_q)
    hot_sibling(7, po, far_q)
    inv = 1.0 / jnp.maximum(jnp.sum(count[...], axis=1, keepdims=True), 1.0)
    invs[...] = jnp.broadcast_to(inv, (DAYS, 128))
    for n in (5, 6, 7, 8):
        ring_b.copies[n].wait_recv()
    for copy in rows + cols + siblings + list(ring_a.copies.values()) + list(ring_b.copies.values()):
        copy.wait_send()


def hbm(x):
    return pltpu.with_memory_space_constraint(x, pltpu.HBM)


HBM = pl.BlockSpec(memory_space=pltpu.HBM)
VMEM = pl.BlockSpec(memory_space=pltpu.VMEM)
DMA = pltpu.SemaphoreType.DMA


def gather(series, day_index, lags):
    return pl.pallas_call(
        gather_kernel,
        out_shape=(
            jax.ShapeDtypeStruct((NCOL, EXT, 128), BF16),
            jax.ShapeDtypeStruct((NCOL, NROW, STEPS, COLW), BF16),
            jax.ShapeDtypeStruct((NLAG, 128), F32),
            jax.ShapeDtypeStruct((2 * DAYS, TIME), BF16),
            jax.ShapeDtypeStruct((TIME, 2 * DAYS), BF16),
            jax.ShapeDtypeStruct((DAYS, 128), F32),
            jax.ShapeDtypeStruct((NCOL, 128), F32),
            jax.ShapeDtypeStruct((128, NCOL), F32),
        ),
        in_specs=[HBM, HBM, HBM],
        out_specs=(VMEM,) * 8,
        scratch_shapes=[
            pltpu.VMEM((DAYS, 128), F32),
            pltpu.VMEM((STEPS, CHANS), BF16),
            pltpu.SMEM((STEPS,), jnp.int32),
            pltpu.SMEM((NLAG,), jnp.int32),
            pltpu.VMEM((NROW, STEPS, ROWW + 128), BF16),
            pltpu.VMEM((NROW, STEPS, ROWW + 128), BF16),
            DMA((3,)),
            DMA((NROW,)),
            DMA((NROW,)),
            DMA((NCOL,)),
            DMA((NCOL,)),
            DMA((9,)),
            DMA((9,)),
            DMA((9,)),
            DMA((9,)),
            DMA((8,)),
            DMA((8,)),
        ],
        compiler_params=pltpu.CompilerParams(
            collective_id=0, has_side_effects=True, vmem_limit_bytes=8 * 2**20
        ),
        name="gather_series",
    )(hbm(series), hbm(day_index), hbm(lags))


def fill(pad, lag, i, held):
    for k in range(NCOL):
        for b in range(NROW):
            to = (k * NROW + b) * 16
            for w in range(3):
                piece = pad[w, pl.ds(PAD + b * 256 + k * 16 + lag, 16), :]
                held[to : to + 16, i * COLW + w * 128 : i * COLW + (w + 1) * 128] = piece.astype(BF16)


def dot(a, b):
    return jnp.dot(a, b, preferred_element_type=F32)


def split(x):
    high = x.astype(BF16)
    return high, (x - high.astype(F32)).astype(BF16)


def cov_kernel(at, bp, lagv, onehot, onehot_t, invs, taper, taper_t, out, anom, pad, early, late, done, sems):
    lag = [jnp.max(lagv[k : k + 1, :]).astype(jnp.int32) for k in range(NLAG)]
    inv_col = invs[:, 0:1]
    inv_row = invs[...].T[0:1, :]
    for k in range(NCOL):
        anom[:, k * 128 : (k + 1) * 128] = at[k, :ROWW, :]

    sums = dot(onehot[:DAYS, :], bp[...].reshape(TIME, COLW))
    both = jnp.concatenate(split(sums * inv_col), axis=0)
    pad[:, :PAD, :] = jnp.zeros((3, PAD, 128), F32)
    pad[:, PAD + TIME :, :] = jnp.zeros((3, PAD, 128), F32)
    for q in range(4):
        season = dot(onehot_t[q * 512 : (q + 1) * 512, :], both)
        for k in range(4 * q, 4 * q + 4):
            here = bp[k].reshape(128, COLW).astype(F32) - season[(k - 4 * q) * 128 : (k - 4 * q + 1) * 128]
            here = (here * taper_t[:, k : k + 1]).astype(BF16).astype(F32)
            for b in range(NROW):
                row = PAD + b * 256 + k * 16
                for w in range(3):
                    pad[w, row : row + 16, :] = here[b * 16 : (b + 1) * 16, w * 128 : (w + 1) * 128]

    sums = lax.dot_general(anom[...], onehot[:DAYS, :], (((1,), (1,)), ((), ())), preferred_element_type=F32)
    both = jnp.concatenate(split(sums * inv_row), axis=1)
    for n in range(4):
        fill(pad, lag[n], n, early)
        season = dot(both, onehot[:, n * 512 : (n + 1) * 512])
        for k in range(4 * n, 4 * n + 4):
            steps = slice(k * 128, (k + 1) * 128)
            here = anom[:, steps].astype(F32) - season[:, (k - 4 * n) * 128 : (k - 4 * n + 1) * 128]
            anom[:, steps] = (here * taper[k : k + 1, :]).astype(BF16)

    copies = []
    for n in range(2 * NPART):
        group, m = divmod(n, NPART)
        slot = n % SLOTS
        if n >= SLOTS:
            copies[n - SLOTS].wait()
        if group == 0:
            for k in range(m * GROUP // NPART, (m + 1) * GROUP // NPART):
                fill(pad, lag[GROUP + k], k, late)
        rows = slice(m * PART, (m + 1) * PART)
        total = dot(anom[rows, :], (early if group == 0 else late)[...]) * (1.0 / TIME)
        for i in range(GROUP):
            done[slot, i] = total[:, i * COLW : (i + 1) * COLW]
        copy = pltpu.make_async_copy(done.at[slot], out.at[group * GROUP : (group + 1) * GROUP, rows], sems.at[slot])
        copy.start()
        copies.append(copy)
    for copy in copies[-SLOTS:]:
        copy.wait()


def covariance(*gathered):
    return pl.pallas_call(
        cov_kernel,
        out_shape=jax.ShapeDtypeStruct((NLAG, ROWW, COLW), F32),
        in_specs=[VMEM] * 8,
        out_specs=HBM,
        scratch_shapes=[
            pltpu.VMEM((ROWW, TIME), BF16),
            pltpu.VMEM((3, TIME + 2 * PAD, 128), F32),
            pltpu.VMEM((TIME, GROUP * COLW), BF16),
            pltpu.VMEM((TIME, GROUP * COLW), BF16),
            pltpu.VMEM((SLOTS, GROUP, PART, COLW), F32),
            DMA((SLOTS,)),
        ],
        compiler_params=pltpu.CompilerParams(vmem_limit_bytes=36 * 2**20),
        name="lagged_covariance",
    )(*gathered)


def shards(series, day_index, lags):
    return covariance(*gather(series, day_index, lags))


def solution(mesh):
    placed = (P(("row", "col"), None), P(("row", "col")), P())
    return jax.shard_map(
        shards, mesh=mesh, in_specs=placed, out_specs=P(None, "row", "col"), check_vma=False
    )
```

```python
import math

import jax
import jax.numpy as jnp
from jax import lax
from jax.experimental import pallas as pl
from jax.experimental.pallas import tpu as pltpu
from jax.sharding import PartitionSpec as P

NLAG = 8
DAYS = 384
TIME = 2048
NROW = 8
NCOL = 16
STEPS = 16
ROWW = 768
COLW = 384
EXT = ROWW + 16
PAD = 32
CHANS = 6144
GROUP = 4
NPART = 2
PART = ROWW // NPART
SLOTS = 3
MESH = pl.DeviceIdType.MESH
F32 = jnp.float32
BF16 = jnp.bfloat16


class Ring:
    def __init__(self, view, half, slot, device, p, q, send, recv):
        self.view, self.half, self.slot, self.device = view, half, slot, device
        self.p, self.q, self.send, self.recv = p, q, send, recv
        self.copies = {}

    def at(self, dq):
        return lax.rem(self.q + dq + 4, 4)

    def copy(self, n, ref, dev):
        copy = pltpu.make_async_remote_copy(
            src_ref=ref,
            dst_ref=ref,
            send_sem=self.send.at[n],
            recv_sem=self.recv.at[n],
            device_id=dev,
            device_id_type=MESH,
        )
        copy.start()
        self.copies[n] = copy

    def own(self):
        ref = self.view(self.slot(self.p, self.q))
        self.copy(1, ref, self.device(self.p, self.at(1)))
        self.copy(2, ref, self.device(self.p, self.at(-1)))
        self.copy(0, ref, self.device(1 - self.p, self.q))

    def other(self):
        self.copies[0].wait_recv()
        ref = self.view(self.slot(1 - self.p, self.q))
        self.copy(3, ref, self.device(self.p, self.at(1)))
        self.copy(4, ref, self.device(self.p, self.at(-1)))

    def forward(self, n):
        self.copies[n].wait_recv()
        pair = self.p if n < 3 else 1 - self.p
        if n % 2 == 1:
            ref = self.half(self.slot(pair, self.at(-1)), 0)
            self.copy(n + 4, ref, self.device(self.p, self.at(1)))
        else:
            ref = self.half(self.slot(pair, self.at(1)), 1)
            self.copy(n + 4, ref, self.device(self.p, self.at(-1)))


def gather_kernel(
    series, days, lags, at, bp, lagv,
    held, held_days, held_lags, stage, land, sl, sa, ra, sb, rb, sra, rra, srb, rrb, ssib, rsib,
):
    r = lax.axis_index("row")
    c = lax.axis_index("col")
    loads = [
        pltpu.make_async_copy(series, held, sl.at[0]),
        pltpu.make_async_copy(days, held_days, sl.at[1]),
        pltpu.make_async_copy(lags, held_lags, sl.at[2]),
    ]
    for load in loads:
        load.start()
    barrier = pltpu.get_barrier_semaphore()
    for j in range(1, NROW):
        pl.semaphore_signal(barrier, inc=1, device_id=(lax.rem(r + j, NROW), c), device_id_type=MESH)
    for j in range(1, NCOL):
        pl.semaphore_signal(barrier, inc=1, device_id=(r, lax.rem(c + j, NCOL)), device_id_type=MESH)

    for load in loads:
        load.wait()
    step = lax.broadcasted_iota(jnp.int32, (STEPS, 128), 0)
    lane = lax.broadcasted_iota(jnp.int32, (STEPS, 128), 1)
    day = jnp.zeros((STEPS, 128), jnp.int32)
    for i in range(STEPS):
        day = jnp.where(step == i, held_days[i], day)
    high = jnp.right_shift(day, 8)
    info = jnp.where(lane == 0, high, jnp.where(lane == 1, day - high * 256, 0))
    info = info.astype(F32).astype(BF16)
    for d in range(NROW):
        stage[d, :, :ROWW] = held[:, d * ROWW : (d + 1) * ROWW]
        stage[d, :, ROWW:] = info

    for k in range(NLAG):
        lagv[k : k + 1, :] = jnp.full((1, 128), held_lags[k], jnp.int32).astype(F32)
    pl.semaphore_wait(barrier, NROW + NCOL - 2)

    rows, cols = [], []
    for j in range(1, NROW):
        to = lax.rem(r + j, NROW)
        copy = pltpu.make_async_remote_copy(
            src_ref=stage.at[to],
            dst_ref=land.at[r],
            send_sem=sa.at[j],
            recv_sem=ra.at[j],
            device_id=(to, c),
            device_id_type=MESH,
        )
        copy.start()
        rows.append(copy)
    for j in range(1, NCOL):
        to = lax.rem(c + j, NCOL)
        copy = pltpu.make_async_remote_copy(
            src_ref=held.at[:, pl.ds(pl.multiple_of(to * COLW, 128), COLW)],
            dst_ref=bp.at[c, r],
            send_sem=sb.at[j],
            recv_sem=rb.at[j],
            device_id=(r, to),
            device_id_type=MESH,
        )
        copy.start()
        cols.append(copy)
    land[r] = stage[r]
    bp[c, r] = held[:, pl.ds(pl.multiple_of(c * COLW, 128), COLW)]

    core = lax.rem(c, 2)
    ring_a = Ring(
        lambda s: at.at[s],
        lambda s, h: at.at[s, 400 * h : 400 + 384 * h],
        lambda p, q: p * 8 + q * 2 + core,
        lambda p, q: (r, p * 8 + q * 2 + core),
        c // 8,
        lax.rem(c // 2, 4),
        sra,
        rra,
    )
    ring_b = Ring(
        lambda s: bp.at[:, s],
        lambda s, h: bp.at[8 * h : 8 * h + 8, s],
        lambda p, q: p * 4 + q,
        lambda p, q: (p * 4 + q, c),
        r // 4,
        lax.rem(r, 4),
        srb,
        rrb,
    )
    siblings = []

    def sibling(p, q):
        n = len(siblings)
        ref = at.at[ring_a.slot(p, q)]
        copy = pltpu.make_async_remote_copy(
            src_ref=ref,
            dst_ref=ref,
            send_sem=ssib.at[n],
            recv_sem=rsib.at[n],
            device_id=(r, c + 1 - 2 * core),
            device_id_type=MESH,
        )
        copy.start()
        siblings.append(copy)

    for copy in rows:
        copy.wait_recv()
    block = land[...].reshape(NROW * STEPS, ROWW + 128).astype(F32)
    at[c] = block.T[:EXT].astype(BF16)
    ring_a.own()
    for copy in cols:
        copy.wait_recv()
    ring_b.own()
    pa, qa = ring_a.p, ring_a.q
    sibling(pa, qa)
    ring_a.other()
    ring_b.other()
    ring_a.forward(1)
    ring_a.forward(2)
    ring_b.forward(1)
    ring_b.forward(2)
    sibling(1 - pa, qa)
    sibling(pa, ring_a.at(-1))
    sibling(pa, ring_a.at(1))
    ring_a.forward(3)
    ring_a.forward(4)
    ring_b.forward(3)
    ring_b.forward(4)
    sibling(1 - pa, ring_a.at(-1))
    sibling(1 - pa, ring_a.at(1))
    for pair, first in ((pa, 5), (1 - pa, 7)):
        ring_a.copies[first].wait_recv()
        ring_a.copies[first + 1].wait_recv()
        sibling(pair, ring_a.at(2))
    for n in (5, 6, 7, 8):
        ring_b.copies[n].wait_recv()
    for copy in siblings:
        copy.wait()
    for copy in rows + cols + list(ring_a.copies.values()) + list(ring_b.copies.values()):
        copy.wait_send()


def hbm(x):
    return pltpu.with_memory_space_constraint(x, pltpu.HBM)


HBM = pl.BlockSpec(memory_space=pltpu.HBM)
VMEM = pl.BlockSpec(memory_space=pltpu.VMEM)
DMA = pltpu.SemaphoreType.DMA


def gather(series, day_index, lags):
    return pl.pallas_call(
        gather_kernel,
        out_shape=(
            jax.ShapeDtypeStruct((NCOL, EXT, 128), BF16),
            jax.ShapeDtypeStruct((NCOL, NROW, STEPS, COLW), BF16),
            jax.ShapeDtypeStruct((NLAG, 128), F32),
        ),
        in_specs=[HBM, HBM, HBM],
        out_specs=(VMEM, VMEM, VMEM),
        scratch_shapes=[
            pltpu.VMEM((STEPS, CHANS), BF16),
            pltpu.SMEM((STEPS,), jnp.int32),
            pltpu.SMEM((NLAG,), jnp.int32),
            pltpu.VMEM((NROW, STEPS, ROWW + 128), BF16),
            pltpu.VMEM((NROW, STEPS, ROWW + 128), BF16),
            DMA((3,)),
            DMA((NROW,)),
            DMA((NROW,)),
            DMA((NCOL,)),
            DMA((NCOL,)),
            DMA((9,)),
            DMA((9,)),
            DMA((9,)),
            DMA((9,)),
            DMA((8,)),
            DMA((8,)),
        ],
        compiler_params=pltpu.CompilerParams(
            collective_id=0, has_side_effects=True, vmem_limit_bytes=8 * 2**20
        ),
        name="gather_series",
    )(hbm(series), hbm(day_index), hbm(lags))


def fill(pad, lag, i, held):
    for b in range(NROW):
        for w in range(3):
            piece = pad[w, pl.ds(PAD + b * 256 + lag, 256), :].astype(BF16)
            for k in range(NCOL):
                to = (k * NROW + b) * 16
                held[to : to + 16, i * COLW + w * 128 : i * COLW + (w + 1) * 128] = piece[k * 16 : (k + 1) * 16]


def dot(a, b):
    return jnp.dot(a, b, preferred_element_type=F32)


def split(x):
    high = x.astype(BF16)
    return high, (x - high.astype(F32)).astype(BF16)


def cov_kernel(lagv, at, bp, out, anom, onehot, onehot_t, pad, early, late, done, sems):
    lag = [jnp.max(lagv[k : k + 1, :]).astype(jnp.int32) for k in range(NLAG)]
    place = lax.broadcasted_iota(jnp.int32, (NCOL, 128), 1)
    when = place // STEPS * (NCOL * STEPS) + lax.broadcasted_iota(jnp.int32, (NCOL, 128), 0) * STEPS + place % STEPS
    taper = 0.5 - 0.5 * jnp.cos(2.0 * math.pi * (when.astype(F32) + 0.5) / TIME)
    taper_t = taper.T

    info = at[:, ROWW:, :].astype(F32)
    day = info[:, 0, :] * 256.0 + info[:, 1, :]
    day_t = day.T
    down = lax.broadcasted_iota(jnp.int32, (DAYS, 128), 0).astype(F32)
    along = lax.broadcasted_iota(jnp.int32, (128, DAYS), 1).astype(F32)
    count = jnp.zeros((DAYS, 128), F32)
    for k in range(NCOL):
        steps = slice(k * 128, (k + 1) * 128)
        anom[:, steps] = at[k, :ROWW, :]
        here = jnp.where(down == day[k : k + 1, :], 1.0, 0.0)
        count = count + here
        hot = here.astype(BF16)
        onehot[:DAYS, steps] = hot
        onehot[DAYS:, steps] = hot
        hot = jnp.where(along == day_t[:, k : k + 1], 1.0, 0.0).astype(BF16)
        onehot_t[steps, :DAYS] = hot
        onehot_t[steps, DAYS:] = hot
    inv_col = 1.0 / jnp.maximum(jnp.sum(count, axis=1, keepdims=True), 1.0)
    inv_row = jnp.broadcast_to(inv_col, (DAYS, 128)).T[0:1, :]

    sums = dot(onehot[:DAYS, :], bp[...].reshape(TIME, COLW))
    both = jnp.concatenate(split(sums * inv_col), axis=0)
    pad[:, :PAD, :] = jnp.zeros((3, PAD, 128), F32)
    pad[:, PAD + TIME :, :] = jnp.zeros((3, PAD, 128), F32)
    for q in range(4):
        season = dot(onehot_t[q * 512 : (q + 1) * 512, :], both)
        for k in range(4 * q, 4 * q + 4):
            here = bp[k].reshape(128, COLW).astype(F32) - season[(k - 4 * q) * 128 : (k - 4 * q + 1) * 128]
            here = (here * taper_t[:, k : k + 1]).astype(BF16).astype(F32)
            for b in range(NROW):
                row = PAD + b * 256 + k * 16
                for w in range(3):
                    pad[w, row : row + 16, :] = here[b * 16 : (b + 1) * 16, w * 128 : (w + 1) * 128]

    fill(pad, lag[0], 0, early)
    fill(pad, lag[1], 1, early)
    sums = lax.dot_general(anom[...], onehot[:DAYS, :], (((1,), (1,)), ((), ())), preferred_element_type=F32)
    both = jnp.concatenate(split(sums * inv_row), axis=1)
    for n in range(4):
        if n < 2:
            fill(pad, lag[n + 2], n + 2, early)
        season = dot(both, onehot[:, n * 512 : (n + 1) * 512])
        for k in range(4 * n, 4 * n + 4):
            steps = slice(k * 128, (k + 1) * 128)
            here = anom[:, steps].astype(F32) - season[:, (k - 4 * n) * 128 : (k - 4 * n + 1) * 128]
            anom[:, steps] = (here * taper[k : k + 1, :]).astype(BF16)

    copies = []
    for n in range(2 * NPART):
        group, m = divmod(n, NPART)
        slot = n % SLOTS
        if n >= SLOTS:
            copies[n - SLOTS].wait()
        if group == 0:
            for k in range(m * GROUP // NPART, (m + 1) * GROUP // NPART):
                fill(pad, lag[GROUP + k], k, late)
        rows = slice(m * PART, (m + 1) * PART)
        total = dot(anom[rows, :], (early if group == 0 else late)[...]) * (1.0 / TIME)
        for i in range(GROUP):
            done[slot, i] = total[:, i * COLW : (i + 1) * COLW]
        copy = pltpu.make_async_copy(done.at[slot], out.at[group * GROUP : (group + 1) * GROUP, rows], sems.at[slot])
        copy.start()
        copies.append(copy)
    for copy in copies[-SLOTS:]:
        copy.wait()


def covariance(at, bp, lagv):
    return pl.pallas_call(
        cov_kernel,
        out_shape=jax.ShapeDtypeStruct((NLAG, ROWW, COLW), F32),
        in_specs=[VMEM] * 3,
        out_specs=HBM,
        scratch_shapes=[
            pltpu.VMEM((ROWW, TIME), BF16),
            pltpu.VMEM((2 * DAYS, TIME), BF16),
            pltpu.VMEM((TIME, 2 * DAYS), BF16),
            pltpu.VMEM((3, TIME + 2 * PAD, 128), F32),
            pltpu.VMEM((TIME, GROUP * COLW), BF16),
            pltpu.VMEM((TIME, GROUP * COLW), BF16),
            pltpu.VMEM((SLOTS, GROUP, PART, COLW), F32),
            DMA((SLOTS,)),
        ],
        compiler_params=pltpu.CompilerParams(vmem_limit_bytes=48 * 2**20),
        name="lagged_covariance",
    )(lagv, at, bp)


def shards(series, day_index, lags):
    return covariance(*gather(series, day_index, lags))


def solution(mesh):
    placed = (P(("row", "col"), None), P(("row", "col")), P())
    return jax.shard_map(
        shards, mesh=mesh, in_specs=placed, out_specs=P(None, "row", "col"), check_vma=False
    )
```

```python
import math

import jax
import jax.numpy as jnp
from jax import lax
from jax.experimental import pallas as pl
from jax.experimental.pallas import tpu as pltpu
from jax.sharding import PartitionSpec as P

NLAG = 8
DAYS = 384
TIME = 2048
NROW = 8
NCOL = 16
STEPS = 16
ROWW = 768
COLW = 384
EXT = ROWW + 16
PAD = 32
CHANS = 6144
GROUP = 4
NPART = 2
PART = ROWW // NPART
SLOTS = 3
MESH = pl.DeviceIdType.MESH
F32 = jnp.float32
BF16 = jnp.bfloat16


class Ring:
    def __init__(self, view, half, slot, device, p, q, send, recv):
        self.view, self.half, self.slot, self.device = view, half, slot, device
        self.p, self.q, self.send, self.recv = p, q, send, recv
        self.copies = {}

    def at(self, dq):
        return lax.rem(self.q + dq + 4, 4)

    def copy(self, n, ref, dev):
        copy = pltpu.make_async_remote_copy(
            src_ref=ref,
            dst_ref=ref,
            send_sem=self.send.at[n],
            recv_sem=self.recv.at[n],
            device_id=dev,
            device_id_type=MESH,
        )
        copy.start()
        self.copies[n] = copy

    def own(self):
        ref = self.view(self.slot(self.p, self.q))
        self.copy(1, ref, self.device(self.p, self.at(1)))
        self.copy(2, ref, self.device(self.p, self.at(-1)))
        self.copy(0, ref, self.device(1 - self.p, self.q))

    def other(self):
        self.copies[0].wait_recv()
        ref = self.view(self.slot(1 - self.p, self.q))
        self.copy(3, ref, self.device(self.p, self.at(1)))
        self.copy(4, ref, self.device(self.p, self.at(-1)))

    def forward(self, n):
        self.copies[n].wait_recv()
        pair = self.p if n < 3 else 1 - self.p
        if n % 2 == 1:
            ref = self.half(self.slot(pair, self.at(-1)), 0)
            self.copy(n + 4, ref, self.device(self.p, self.at(1)))
        else:
            ref = self.half(self.slot(pair, self.at(1)), 1)
            self.copy(n + 4, ref, self.device(self.p, self.at(-1)))


def gather_kernel(
    series, days, lags, at, bp, lagv,
    held, held_days, held_lags, stage, land, sl, sa, ra, sb, rb, sra, rra, srb, rrb, ssib, rsib,
):
    r = lax.axis_index("row")
    c = lax.axis_index("col")
    loads = [
        pltpu.make_async_copy(series, held, sl.at[0]),
        pltpu.make_async_copy(days, held_days, sl.at[1]),
        pltpu.make_async_copy(lags, held_lags, sl.at[2]),
    ]
    for load in loads:
        load.start()
    barrier = pltpu.get_barrier_semaphore()
    for j in range(1, NROW):
        pl.semaphore_signal(barrier, inc=1, device_id=(lax.rem(r + j, NROW), c), device_id_type=MESH)
    for j in range(1, NCOL):
        pl.semaphore_signal(barrier, inc=1, device_id=(r, lax.rem(c + j, NCOL)), device_id_type=MESH)

    for load in loads:
        load.wait()
    step = lax.broadcasted_iota(jnp.int32, (STEPS, 128), 0)
    lane = lax.broadcasted_iota(jnp.int32, (STEPS, 128), 1)
    day = jnp.zeros((STEPS, 128), jnp.int32)
    for i in range(STEPS):
        day = jnp.where(step == i, held_days[i], day)
    high = jnp.right_shift(day, 8)
    info = jnp.where(lane == 0, high, jnp.where(lane == 1, day - high * 256, 0))
    info = info.astype(F32).astype(BF16)
    for d in range(NROW):
        stage[d, :, :ROWW] = held[:, d * ROWW : (d + 1) * ROWW]
        stage[d, :, ROWW:] = info

    for k in range(NLAG):
        lagv[k : k + 1, :] = jnp.full((1, 128), held_lags[k], jnp.int32).astype(F32)
    pl.semaphore_wait(barrier, NROW + NCOL - 2)

    rows, cols = [], []
    for j in range(1, NROW):
        to = lax.rem(r + j, NROW)
        copy = pltpu.make_async_remote_copy(
            src_ref=stage.at[to],
            dst_ref=land.at[r],
            send_sem=sa.at[j],
            recv_sem=ra.at[j],
            device_id=(to, c),
            device_id_type=MESH,
        )
        copy.start()
        rows.append(copy)
    for j in range(1, NCOL):
        to = lax.rem(c + j, NCOL)
        copy = pltpu.make_async_remote_copy(
            src_ref=held.at[:, pl.ds(pl.multiple_of(to * COLW, 128), COLW)],
            dst_ref=bp.at[c, r],
            send_sem=sb.at[j],
            recv_sem=rb.at[j],
            device_id=(r, to),
            device_id_type=MESH,
        )
        copy.start()
        cols.append(copy)
    land[r] = stage[r]
    bp[c, r] = held[:, pl.ds(pl.multiple_of(c * COLW, 128), COLW)]

    core = lax.rem(c, 2)
    ring_a = Ring(
        lambda s: at.at[s],
        lambda s, h: at.at[s, 400 * h : 400 + 384 * h],
        lambda p, q: p * 8 + q * 2 + core,
        lambda p, q: (r, p * 8 + q * 2 + core),
        c // 8,
        lax.rem(c // 2, 4),
        sra,
        rra,
    )
    ring_b = Ring(
        lambda s: bp.at[:, s],
        lambda s, h: bp.at[8 * h : 8 * h + 8, s],
        lambda p, q: p * 4 + q,
        lambda p, q: (p * 4 + q, c),
        r // 4,
        lax.rem(r, 4),
        srb,
        rrb,
    )
    siblings = []

    def sibling(p, q):
        n = len(siblings)
        ref = at.at[ring_a.slot(p, q)]
        copy = pltpu.make_async_remote_copy(
            src_ref=ref,
            dst_ref=ref,
            send_sem=ssib.at[n],
            recv_sem=rsib.at[n],
            device_id=(r, c + 1 - 2 * core),
            device_id_type=MESH,
        )
        copy.start()
        siblings.append(copy)

    for copy in rows:
        copy.wait_recv()
    block = land[...].reshape(NROW * STEPS, ROWW + 128).astype(F32)
    at[c] = block.T[:EXT].astype(BF16)
    ring_a.own()
    for copy in cols:
        copy.wait_recv()
    ring_b.own()
    pa, qa = ring_a.p, ring_a.q
    sibling(pa, qa)
    ring_a.other()
    ring_b.other()
    ring_a.forward(1)
    ring_a.forward(2)
    ring_b.forward(1)
    ring_b.forward(2)
    sibling(1 - pa, qa)
    sibling(pa, ring_a.at(-1))
    sibling(pa, ring_a.at(1))
    for n in (5, 6):
        ring_a.copies[n].wait_recv()
    ring_a.copy(7, ring_a.view(ring_a.slot(pa, ring_a.at(2))), ring_a.device(1 - pa, qa))
    sibling(pa, ring_a.at(2))
    for n in (3, 4):
        ring_a.copies[n].wait_recv()
        ring_b.forward(n)
    sibling(1 - pa, ring_a.at(-1))
    sibling(1 - pa, ring_a.at(1))
    ring_a.copies[7].wait_recv()
    sibling(1 - pa, ring_a.at(2))
    for n in (5, 6, 7, 8):
        ring_b.copies[n].wait_recv()
    for copy in siblings:
        copy.wait()
    for copy in rows + cols + list(ring_a.copies.values()) + list(ring_b.copies.values()):
        copy.wait_send()


def hbm(x):
    return pltpu.with_memory_space_constraint(x, pltpu.HBM)


HBM = pl.BlockSpec(memory_space=pltpu.HBM)
VMEM = pl.BlockSpec(memory_space=pltpu.VMEM)
DMA = pltpu.SemaphoreType.DMA


def gather(series, day_index, lags):
    return pl.pallas_call(
        gather_kernel,
        out_shape=(
            jax.ShapeDtypeStruct((NCOL, EXT, 128), BF16),
            jax.ShapeDtypeStruct((NCOL, NROW, STEPS, COLW), BF16),
            jax.ShapeDtypeStruct((NLAG, 128), F32),
        ),
        in_specs=[HBM, HBM, HBM],
        out_specs=(VMEM, VMEM, VMEM),
        scratch_shapes=[
            pltpu.VMEM((STEPS, CHANS), BF16),
            pltpu.SMEM((STEPS,), jnp.int32),
            pltpu.SMEM((NLAG,), jnp.int32),
            pltpu.VMEM((NROW, STEPS, ROWW + 128), BF16),
            pltpu.VMEM((NROW, STEPS, ROWW + 128), BF16),
            DMA((3,)),
            DMA((NROW,)),
            DMA((NROW,)),
            DMA((NCOL,)),
            DMA((NCOL,)),
            DMA((9,)),
            DMA((9,)),
            DMA((9,)),
            DMA((9,)),
            DMA((8,)),
            DMA((8,)),
        ],
        compiler_params=pltpu.CompilerParams(
            collective_id=0, has_side_effects=True, vmem_limit_bytes=8 * 2**20
        ),
        name="gather_series",
    )(hbm(series), hbm(day_index), hbm(lags))


def fill(pad, lag, i, held):
    for b in range(NROW):
        for w in range(3):
            piece = pad[w, pl.ds(PAD + b * 256 + lag, 256), :].astype(BF16)
            for k in range(NCOL):
                to = (k * NROW + b) * 16
                held[to : to + 16, i * COLW + w * 128 : i * COLW + (w + 1) * 128] = piece[k * 16 : (k + 1) * 16]


def dot(a, b):
    return jnp.dot(a, b, preferred_element_type=F32)


def split(x):
    high = x.astype(BF16)
    return high, (x - high.astype(F32)).astype(BF16)


def cov_kernel(lagv, at, bp, out, anom, onehot, onehot_t, pad, early, late, done, sems):
    lag = [jnp.max(lagv[k : k + 1, :]).astype(jnp.int32) for k in range(NLAG)]
    place = lax.broadcasted_iota(jnp.int32, (NCOL, 128), 1)
    when = place // STEPS * (NCOL * STEPS) + lax.broadcasted_iota(jnp.int32, (NCOL, 128), 0) * STEPS + place % STEPS
    taper = 0.5 - 0.5 * jnp.cos(2.0 * math.pi * (when.astype(F32) + 0.5) / TIME)
    taper_t = taper.T

    info = at[:, ROWW:, :].astype(F32)
    day = info[:, 0, :] * 256.0 + info[:, 1, :]
    day_t = day.T
    down = lax.broadcasted_iota(jnp.int32, (DAYS, 128), 0).astype(F32)
    along = lax.broadcasted_iota(jnp.int32, (128, DAYS), 1).astype(F32)
    count = jnp.zeros((DAYS, 128), F32)
    for k in range(NCOL):
        steps = slice(k * 128, (k + 1) * 128)
        anom[:, steps] = at[k, :ROWW, :]
        here = jnp.where(down == day[k : k + 1, :], 1.0, 0.0)
        count = count + here
        hot = here.astype(BF16)
        onehot[:DAYS, steps] = hot
        onehot[DAYS:, steps] = hot
        hot = jnp.where(along == day_t[:, k : k + 1], 1.0, 0.0).astype(BF16)
        onehot_t[steps, :DAYS] = hot
        onehot_t[steps, DAYS:] = hot
    inv_col = 1.0 / jnp.maximum(jnp.sum(count, axis=1, keepdims=True), 1.0)
    inv_row = jnp.broadcast_to(inv_col, (DAYS, 128)).T[0:1, :]

    sums = dot(onehot[:DAYS, :], bp[...].reshape(TIME, COLW))
    both = jnp.concatenate(split(sums * inv_col), axis=0)
    pad[:, :PAD, :] = jnp.zeros((3, PAD, 128), F32)
    pad[:, PAD + TIME :, :] = jnp.zeros((3, PAD, 128), F32)
    for q in range(4):
        season = dot(onehot_t[q * 512 : (q + 1) * 512, :], both)
        for k in range(4 * q, 4 * q + 4):
            here = bp[k].reshape(128, COLW).astype(F32) - season[(k - 4 * q) * 128 : (k - 4 * q + 1) * 128]
            here = (here * taper_t[:, k : k + 1]).astype(BF16).astype(F32)
            for b in range(NROW):
                row = PAD + b * 256 + k * 16
                for w in range(3):
                    pad[w, row : row + 16, :] = here[b * 16 : (b + 1) * 16, w * 128 : (w + 1) * 128]

    fill(pad, lag[0], 0, early)
    fill(pad, lag[1], 1, early)
    sums = lax.dot_general(anom[...], onehot[:DAYS, :], (((1,), (1,)), ((), ())), preferred_element_type=F32)
    both = jnp.concatenate(split(sums * inv_row), axis=1)
    for n in range(4):
        if n < 2:
            fill(pad, lag[n + 2], n + 2, early)
        season = dot(both, onehot[:, n * 512 : (n + 1) * 512])
        for k in range(4 * n, 4 * n + 4):
            steps = slice(k * 128, (k + 1) * 128)
            here = anom[:, steps].astype(F32) - season[:, (k - 4 * n) * 128 : (k - 4 * n + 1) * 128]
            anom[:, steps] = (here * taper[k : k + 1, :]).astype(BF16)

    copies = []
    for n in range(2 * NPART):
        group, m = divmod(n, NPART)
        slot = n % SLOTS
        if n >= SLOTS:
            copies[n - SLOTS].wait()
        if group == 0:
            for k in range(m * GROUP // NPART, (m + 1) * GROUP // NPART):
                fill(pad, lag[GROUP + k], k, late)
        rows = slice(m * PART, (m + 1) * PART)
        total = dot(anom[rows, :], (early if group == 0 else late)[...]) * (1.0 / TIME)
        for i in range(GROUP):
            done[slot, i] = total[:, i * COLW : (i + 1) * COLW]
        copy = pltpu.make_async_copy(done.at[slot], out.at[group * GROUP : (group + 1) * GROUP, rows], sems.at[slot])
        copy.start()
        copies.append(copy)
    for copy in copies[-SLOTS:]:
        copy.wait()


def covariance(at, bp, lagv):
    return pl.pallas_call(
        cov_kernel,
        out_shape=jax.ShapeDtypeStruct((NLAG, ROWW, COLW), F32),
        in_specs=[VMEM] * 3,
        out_specs=HBM,
        scratch_shapes=[
            pltpu.VMEM((ROWW, TIME), BF16),
            pltpu.VMEM((2 * DAYS, TIME), BF16),
            pltpu.VMEM((TIME, 2 * DAYS), BF16),
            pltpu.VMEM((3, TIME + 2 * PAD, 128), F32),
            pltpu.VMEM((TIME, GROUP * COLW), BF16),
            pltpu.VMEM((TIME, GROUP * COLW), BF16),
            pltpu.VMEM((SLOTS, GROUP, PART, COLW), F32),
            DMA((SLOTS,)),
        ],
        compiler_params=pltpu.CompilerParams(vmem_limit_bytes=48 * 2**20),
        name="lagged_covariance",
    )(lagv, at, bp)


def shards(series, day_index, lags):
    return covariance(*gather(series, day_index, lags))


def solution(mesh):
    placed = (P(("row", "col"), None), P(("row", "col")), P())
    return jax.shard_map(
        shards, mesh=mesh, in_specs=placed, out_specs=P(None, "row", "col"), check_vma=False
    )
```
